32 devices in a mesh: tile: 8 (over y, x, core), wave: 4 (over z).
Axes of the slice: x: 2, y: 2, z: 4, core: 2. Of those that a mesh axis runs over, the one named last changes fastest.
Arguments:
- maps: float32 [4, 128, 1024], P(None, None, 'tile'), may hold values from 0 to 2
- measured: float32 [16, 128, 128], P('tile'), may hold values from 0 to 8
- offsets: int32 [16], P('tile'), may hold values from -64 to 64, as said below
- probe: float32 [48, 2, 128, 128], P('wave'), may hold values from -6 to 6
- spectrum: float32 [48], P('wave'), may hold values from 0.05 to 0.5
- wave_index: int32 [48], P('wave'), may hold values from 0 to 47, each once
- edge_band: int32 [48, 4], P('wave'), may hold values from 0 to 2
- band_coef: float32 [2, 3, 4], replicated, may hold values from 0.1 to 0.8
Outputs:
- new_maps: float32 [4, 128, 1024], P(None, None, 'tile')
The draws below stay inside these ranges and needn't reach their ends.
Inputs may be any that keep to these rules, and one draw needn't show every extreme that they name: `offsets`: a frame reaches at most 64 columns into either neighbouring tile; in every tile one frame starts exactly 64 columns before the tile and another ends exactly 64 columns after it. `wave_index`: each wavelength is held by exactly one slot.
All inputs are finite; a program needn't handle non-finite values.
Results may differ from the reference program's by a relative error of at most 0.0024.
Values sent between devices are 32-bit elements; how exact they have to be, the bound alone decides.
No kernel may reach another device: no remote copies, remote signals or barrier semaphores. Data moves between devices by JAX's collectives and lax.ppermute only.
A program may use at most 64 MiB of HBM per device.

```python
import math
import jax
import jax.numpy as jnp
from jax import lax

FRAME = 128
COLS = 128
FRAMES = 2
WAVES = 48
MATERIALS = 4
BANDS = 3
TILECOLS = 1024
FRAMES_ALL = 16
N_TILE = 8


def draw_maps(key, part):
    base = jax.random.uniform(jax.random.fold_in(key, 11), (MATERIALS, FRAME, TILECOLS), jnp.float32)
    position = jnp.arange(TILECOLS, dtype=jnp.float32) / (TILECOLS - 1)
    thickness = 0.25 + 1.75 * position
    return base * thickness[None, None, :]


def draw_offsets(key, part):
    tiles = FRAMES_ALL // FRAMES
    margin = FRAME // 2
    lowest = 0 - margin
    highest = COLS + margin - FRAME
    spread = jax.random.randint(jax.random.fold_in(key, 21), (tiles, FRAMES), lowest, highest + 1, dtype=jnp.int32)
    first = jax.random.randint(jax.random.fold_in(key, 22), (tiles, 1), 0, FRAMES, dtype=jnp.int32)
    step_on = jax.random.randint(jax.random.fold_in(key, 23), (tiles, 1), 1, FRAMES, dtype=jnp.int32)
    second = (first + step_on) % FRAMES
    slots = jnp.arange(FRAMES, dtype=jnp.int32)[None, :]
    spread = jnp.where(slots == first, lowest, spread)
    spread = jnp.where(slots == second, highest, spread)
    return spread.reshape(FRAMES_ALL).astype(jnp.int32)


def touch_ends(result, own_key, smallest, top_value):
    extent = result.shape
    place = [jax.random.randint(jax.random.fold_in(own_key, axis), (), 0, extent[axis]) for axis in range(len(extent))]
    result = result.at[tuple(place)].set(smallest)
    longest = extent.index(max(extent))
    place[longest] = (place[longest] + 1) % extent[longest]
    return result.at[tuple(place)].set(top_value)


def block_scale(own_key, extent, split, low, largest):
    def one(axis_at, parts):
        steps = jax.random.uniform(jax.random.fold_in(jax.random.fold_in(own_key, 6), axis_at), (parts,), jnp.float32, low / len(split), largest / len(split))
        return jnp.repeat(jnp.exp(steps), extent[axis_at] // parts).reshape((-1,) + (1,) * (len(extent) - axis_at - 1))

    loudness = one(*split[0])
    for cut in split[1:]:
        loudness = loudness * one(*cut)
    return loudness


def gaussian(own_key, extent, deviation, most, pieces=(), kind=jnp.bfloat16):
    factor_of = block_scale(own_key, extent, pieces, -0.22, 0.18) if pieces else 1.0
    array = jax.random.normal(own_key, extent, jnp.float32) * deviation * factor_of
    return jnp.minimum(jnp.maximum(array, -most), most).astype(kind)


def setup_inputs(seed: int = 0) -> dict:
    key_list = jax.random.split(jax.random.key(seed), 9)
    return {
        "maps": draw_maps(jax.random.fold_in(key_list[8], 71), 0),
        "measured": jnp.clip(8.0 * jax.random.uniform(key_list[1], (FRAMES_ALL, FRAME, FRAME), jnp.float32) ** block_scale(key_list[1], (FRAMES_ALL, FRAME, FRAME), ((0, 8),), -0.2, 0.2), 0.0, 8.0),
        "offsets": draw_offsets(jax.random.fold_in(key_list[8], 71), 0),
        "probe": gaussian(key_list[3], (WAVES, 2, FRAME, FRAME), 1.0, 6.0, ((0, 4),), jnp.float32),
        "spectrum": jnp.clip(jnp.exp(math.log(0.5) - 2.3025851 * jax.random.uniform(key_list[4], (WAVES,), jnp.float32) ** block_scale(key_list[4], (WAVES,), ((0, 4),), -0.2, 0.2)), 0.05, 0.5),
        "wave_index": jax.random.permutation(key_list[5], WAVES).astype(jnp.int32),
        "edge_band": touch_ends(jax.random.randint(key_list[6], (WAVES, MATERIALS), 0, BANDS), jax.random.fold_in(key_list[6], 1), 0, BANDS - 1).astype(jnp.int32),
        "band_coef": jnp.clip(jax.random.uniform(key_list[7], (2, BANDS, MATERIALS), jnp.float32, 0.1, 0.8), 0.1, 0.8),
    }


relax = 4.0
floor_level = 1.0

def chirp_table(which_wave, length):
    centred = jnp.arange(length, dtype=jnp.int32) - length // 2
    product = (centred[:, None] * centred[None, :]).astype(jnp.float32)
    sampling = 0.6 + 0.4 * which_wave.astype(jnp.float32) / (WAVES - 1)
    phase_angle = -2.0 * math.pi / length * sampling[..., None, None] * product
    normaliser = 1.0 / math.sqrt(length)
    return ((jnp.cos(phase_angle) * normaliser).astype(jnp.bfloat16), (jnp.sin(phase_angle) * normaliser).astype(jnp.bfloat16))

def left_product(table, data):
    return jnp.einsum('skn,snj->skj', table.astype(jnp.float32), data.astype(jnp.float32), precision=lax.Precision.HIGHEST)

def right_product(data, table):
    return jnp.einsum('skn,snj->skj', data.astype(jnp.float32), table.astype(jnp.float32), precision=lax.Precision.HIGHEST)

def transform(table_re, table_im, data_re, data_im):
    mid_re = (left_product(table_re, data_re) - left_product(table_im, data_im)).astype(jnp.bfloat16)
    mid_im = (left_product(table_re, data_im) + left_product(table_im, data_re)).astype(jnp.bfloat16)
    out_re = right_product(mid_re, table_re) - right_product(mid_im, table_im)
    out_im = right_product(mid_re, table_im) + right_product(mid_im, table_re)
    return (out_re, out_im)

def reference(maps, measured, offsets, probe, spectrum, wave_index, edge_band, band_coef):
    materials = maps.shape[0]
    margin = FRAME // 2
    padded = jnp.pad(maps, ((0, 0), (0, 0), (margin, margin)))
    onehot = (edge_band[:, :, None] == jnp.arange(BANDS, dtype=jnp.int32)).astype(jnp.float32)
    coefficient = jnp.einsum('smb,cbm->csm', onehot, band_coef.astype(jnp.float32), precision=lax.Precision.HIGHEST)
    table_re, table_im = chirp_table(wave_index, FRAME)
    tile_of = jnp.arange(FRAMES * N_TILE, dtype=jnp.int32) // FRAMES
    starts = (tile_of * COLS + offsets + margin).astype(jnp.int32)
    weights = spectrum[:, None, None]

    def frame_step(accumulated, inputs):
        start_col, observed = inputs
        window = lax.dynamic_slice_in_dim(padded, start_col, FRAME, 2)
        absorb = jnp.einsum('sm,mrk->srk', coefficient[0], window, precision=lax.Precision.HIGHEST)
        phase_sum = jnp.einsum('sm,mrk->srk', coefficient[1], window, precision=lax.Precision.HIGHEST)
        damping = jnp.exp(-absorb)
        obj_re = damping * jnp.cos(phase_sum)
        obj_im = damping * jnp.sin(phase_sum)
        psi_re = probe[:, 0] * obj_re - probe[:, 1] * obj_im
        psi_im = probe[:, 0] * obj_im + probe[:, 1] * obj_re
        far_re, far_im = transform(table_re, table_im, psi_re.astype(jnp.bfloat16), psi_im.astype(jnp.bfloat16))
        intensity = lax.optimization_barrier(jnp.sum(weights * (far_re * far_re + far_im * far_im), axis=0))
        shortfall = jnp.sqrt(observed / jnp.maximum(intensity, floor_level)) - 1.0
        factor = weights * shortfall[None]
        back_re, back_im = transform(table_re, -table_im, (factor * far_re).astype(jnp.bfloat16), (factor * far_im).astype(jnp.bfloat16))
        cross_re = psi_re * back_re + psi_im * back_im
        cross_im = psi_re * back_im - psi_im * back_re
        gradient = jnp.einsum('sm,skj->mkj', -coefficient[0], cross_re, precision=lax.Precision.HIGHEST) + jnp.einsum('sm,skj->mkj', coefficient[1], cross_im, precision=lax.Precision.HIGHEST)
        power_sum = lax.optimization_barrier(jnp.sum(weights * (psi_re * psi_re + psi_im * psi_im), axis=0))
        term = jnp.concatenate([gradient, power_sum[None]], axis=0)
        current = lax.dynamic_slice_in_dim(accumulated, start_col, FRAME, 2)
        accumulated = lax.dynamic_update_slice_in_dim(accumulated, current + term, start_col, 2)
        return (accumulated, None)
    accumulated = jnp.zeros((materials + 1, FRAME, COLS * N_TILE + 2 * margin), jnp.float32)
    accumulated, _ = lax.scan(frame_step, accumulated, (starts, measured))
    reduced = accumulated[:, :, margin:margin + COLS * N_TILE]
    return maps + relax * reduced[:materials] / (reduced[materials] + 1.0)
```

```python
import math

import jax
import jax.numpy as jnp
import numpy as np
from jax import lax
from jax.experimental import pallas as pl
from jax.experimental.pallas import tpu as pltpu
from jax.sharding import PartitionSpec as P

WAVES = 48

relax = 4.0
floor_level = 1.0

VM = pl.BlockSpec(memory_space=pltpu.VMEM)
SM = pl.BlockSpec(memory_space=pltpu.SMEM)
f32 = jnp.float32
bf16 = jnp.bfloat16


def fit(parity, degree):
    nodes = 0.5 * np.cos(np.pi * (np.arange(400) + 0.5) / 800)
    turns = 2 * np.pi * nodes
    value = np.sin(turns) if parity else np.cos(turns)
    powers = np.stack([nodes ** (parity + 2 * i) for i in range(degree)], axis=1)
    return [float(c) for c in np.linalg.lstsq(powers, value, rcond=None)[0]]


SIN = fit(1, 6)
COS = fit(0, 7)


def horner(square, coefs):
    total = coefs[-1]
    for c in coefs[-2::-1]:
        total = total * square + c
    return total


def cos_sin(turns):
    r = turns - jnp.round(turns)
    square = r * r
    return horner(square, COS), horner(square, SIN) * r


def lanes(rows, length):
    return lax.broadcasted_iota(jnp.int32, (rows, length), 1)


def halves_packed(top, bottom, upper):
    length = top.shape[-1]
    half = length // 2
    low = lanes(top.shape[0], length) < half
    if upper:
        return jnp.where(low, pltpu.roll(top, half, 1), bottom)
    return jnp.where(low, top, pltpu.roll(bottom, half, 1))


def block(table_ref, s, kind):
    re, im, neg = table_ref[s, 0], table_ref[s, 1], table_ref[s, 2]
    top, bottom = ((re, neg), (im, re)) if kind == "L" else ((re, im), (neg, re))
    return jnp.concatenate(
        [jnp.concatenate(top, axis=1), jnp.concatenate(bottom, axis=1)], axis=0
    )


def transform(left, right, re, im):
    length = re.shape[0]
    stacked = jnp.concatenate([re.astype(bf16), im.astype(bf16)], axis=0)
    mid = jnp.dot(left, stacked, preferred_element_type=f32).astype(bf16)
    beside = jnp.concatenate([mid[:length], mid[length:]], axis=1)
    return jnp.dot(beside, right, preferred_element_type=f32)


def pack_kernel(offsets, maps, measured, out):
    materials, length, _ = maps.shape
    half = length // 2
    for m in range(materials):
        out[m * half : (m + 1) * half] = halves_packed(maps[m, :half], maps[m, half:], False)
    left = jnp.where(offsets[0] < offsets[1], 0, 1)
    out[materials * half :] = measured[left]


def first_kernel(tiles, spectrum, wave_index, edge_band, band_coef, maps, probe, table, power):
    materials, length, _ = maps.shape
    half = length // 2
    slots = probe.shape[0]
    tile = lax.axis_index("tile")
    group = 8
    centred_lane = (lanes(group, length) - half).astype(f32)
    row = lax.broadcasted_iota(jnp.int32, (group, length), 0)
    fine = row.astype(f32) * centred_lane / length
    normaliser = 1.0 / math.sqrt(length)
    coarse_rows = length // group

    def tables(s, carry):
        which = jnp.full((group, length), wave_index[s], jnp.int32).astype(f32)
        sampling = 0.6 + 0.4 * which / (WAVES - 1)
        fine_cos, fine_sin = cos_sin(sampling * fine)
        fine_cos, fine_sin = fine_cos * normaliser, fine_sin * normaliser
        for base in range(0, coarse_rows, group):
            step = ((row + base) * group - half).astype(f32) * centred_lane / length
            cos, sin = cos_sin(sampling * step)
            for i in range(0, group, 2):
                parts = []
                for j in (i, i + 1):
                    c = jnp.broadcast_to(cos[j : j + 1], (group, length))
                    n = jnp.broadcast_to(sin[j : j + 1], (group, length))
                    parts.append((c * fine_cos - n * fine_sin, n * fine_cos + c * fine_sin))
                at = pl.ds((base + i) * group, 2 * group)
                re = jnp.concatenate([parts[0][0], parts[1][0]], axis=0).astype(bf16)
                positive = jnp.concatenate([parts[0][1], parts[1][1]], axis=0)
                table[s, 0, at, :] = re
                table[s, 1, at, :] = (-positive).astype(bf16)
                table[s, 2, at, :] = positive.astype(bf16)
        return carry

    lax.fori_loop(0, slots, tables, 0)

    chunk = 32
    low = lanes(chunk, length) < half
    frames = jnp.where(
        low,
        jnp.where(tile == tiles - 1, 1.0, 2.0),
        jnp.where(tile == 0, 1.0, 2.0),
    )
    for start in range(0, length, chunk):
        at = slice(start, start + chunk)
        own = [pltpu.roll(maps[m, at], half, 1) for m in range(materials)]

        def add(s, total):
            absorb = None
            for m in range(materials):
                coef = band_coef[0, edge_band[s, m], m] * (-2.0 * math.log2(math.e))
                absorb = coef * own[m] if absorb is None else absorb + coef * own[m]
            re, im = probe[s, 0, at], probe[s, 1, at]
            return total + (spectrum[s] * jnp.exp2(absorb)) * (re * re + im * im)

        total = lax.fori_loop(0, slots, add, jnp.zeros((chunk, length), f32))
        power[at] = frames * total


def piece(array, q, count, half_rows):
    groups = count // 2
    rows = 2 * half_rows
    start = pl.multiple_of(lax.rem(q, groups) * rows, half_rows)
    top = array[pl.ds(start, half_rows), :]
    bottom = array[pl.ds(start + half_rows, half_rows), :]
    return jnp.where(
        q < groups, halves_packed(top, bottom, False), halves_packed(top, bottom, True)
    )


def forward_kernel(
    tiles, count, spectrum, edge_band, band_coef, maps, halo, probe, table, power,
    psi, far, far_edge, keep, edge_keep, *messages_and_scratch,
):
    messages = messages_and_scratch[: count - 1]
    window, total, total_edge = messages_and_scratch[count - 1 :]
    materials, length, _ = maps.shape
    half = length // 2
    slots = probe.shape[0]
    edge = lax.axis_index("tile") == tiles - 1
    me = lax.axis_index("wave")
    low = lanes(half, length) < half
    for m in range(materials):
        packed = halo[m * half : (m + 1) * half]
        window[m, :half] = jnp.where(
            low, pltpu.roll(maps[m, :half], half, 1), pltpu.roll(packed, half, 1)
        )
        window[m, half:] = jnp.where(low, pltpu.roll(maps[m, half:], half, 1), packed)
    total[...] = jnp.zeros_like(total)
    chunk = 32

    def exit_wave(s):
        for start in range(0, length, chunk):
            at = slice(start, start + chunk)
            absorb, phase = None, None
            for m in range(materials):
                band = edge_band[s, m]
                a = band_coef[0, band, m] * (-math.log2(math.e))
                b = band_coef[1, band, m] * (0.5 / math.pi)
                w = window[m, at]
                absorb = a * w if absorb is None else absorb + a * w
                phase = b * w if phase is None else phase + b * w
            damping = jnp.exp2(absorb)
            cos, sin = cos_sin(phase)
            cos, sin = damping * cos, damping * sin
            re, im = probe[s, 0, at], probe[s, 1, at]
            psi[s, 0, at] = re * cos - im * sin
            psi[s, 1, at] = re * sin + im * cos

    def add_intensity(s, got, total):
        re, im = got[:, :length], got[:, length:]
        total[...] += spectrum[s] * (re * re + im * im)

    @pl.when(jnp.logical_not(edge))
    def _():
        def step(s, carry):
            exit_wave(s)
            got = transform(block(table, s, "L"), block(table, s, "R"), psi[s, 0], psi[s, 1])
            far[s] = got
            add_intensity(s, got, total)
            return carry

        lax.fori_loop(0, slots, step, 0)

    @pl.when(edge)
    def _():
        total_edge[...] = jnp.zeros_like(total_edge)
        low = lanes(length, length) < half

        def step(s, carry):
            exit_wave(s)
            left, right = block(table, s, "L"), block(table, s, "R")
            re, im, bare_re, bare_im = psi[s, 0], psi[s, 1], probe[s, 0], probe[s, 1]
            got = transform(left, right, jnp.where(low, re, bare_re), jnp.where(low, im, bare_im))
            far[s] = got
            add_intensity(s, got, total)
            got = transform(left, right, jnp.where(low, bare_re, re), jnp.where(low, bare_im, im))
            far_edge[s] = got
            add_intensity(s, got, total_edge)
            return carry

        lax.fori_loop(0, slots, step, 0)
        edge_keep[...] = total_edge[...]

    half_rows = length // count
    for k, message in enumerate((keep, *messages)):
        message[:length] = total[...]
        message[length:] = piece(power, lax.rem(me + k, count), count, half_rows)


def backward_kernel(
    tiles, count, offsets, spectrum, edge_band, band_coef, measured, halo, table, psi, far, far_edge,
    *rest,
):
    shares, rest = rest[:count], rest[count:]
    edges, rest = rest[:count], rest[count:]
    sends, rest = rest[:count], rest[count:]
    power, shortfall, shortfall_edge, gradient, back = rest
    materials = edge_band.shape[1]
    length = measured.shape[1]
    half = length // 2
    slots = psi.shape[0]
    edge = lax.axis_index("tile") == tiles - 1
    me = lax.axis_index("wave")
    half_rows = length // count
    intensity = shares[0][:length]
    powers = shares[0][length:]
    for share in shares[1:]:
        intensity = intensity + share[:length]
        powers = powers + share[length:]
    power[...] = relax / (powers + 1.0)
    mine = jnp.sqrt(measured[jnp.where(offsets[0] < offsets[1], 1, 0)])
    theirs = jnp.sqrt(halo[materials * half :])
    inverse = lax.rsqrt(jnp.maximum(intensity, floor_level))
    gradient[...] = jnp.zeros_like(gradient)

    def delta(s, far, shortfall):
        factor = spectrum[s] * shortfall[...]
        return factor * far[s, :, :length], factor * far[s, :, length:]

    chunk = 32

    def collect(s):
        for start in range(0, length, chunk):
            at = slice(start, start + chunk)
            re, im = psi[s, 0, at], psi[s, 1, at]
            back_re, back_im = back[at, :length], back[at, length:]
            cross_re = re * back_re + im * back_im
            cross_im = re * back_im - im * back_re
            for m in range(materials):
                band = edge_band[s, m]
                gradient[m, at] += band_coef[1, band, m] * cross_im - band_coef[0, band, m] * cross_re

    @pl.when(jnp.logical_not(edge))
    def _():
        shortfall[...] = (mine + theirs) * inverse - 2.0

        def step(s, carry):
            back[...] = transform(block(table, s, "R"), block(table, s, "L"), *delta(s, far, shortfall))
            collect(s)
            return carry

        lax.fori_loop(0, slots, step, 0)

    @pl.when(edge)
    def _():
        shortfall[...] = mine * inverse - 1.0
        intensity = edges[0][...]
        for share in edges[1:]:
            intensity = intensity + share[...]
        shortfall_edge[...] = theirs * lax.rsqrt(jnp.maximum(intensity, floor_level)) - 1.0
        low = (lax.broadcasted_iota(jnp.int32, (length, 2 * length), 1) & (length - 1)) < half

        def step(s, carry):
            left, right = block(table, s, "R"), block(table, s, "L")
            one = transform(left, right, *delta(s, far, shortfall))
            two = transform(left, right, *delta(s, far_edge, shortfall_edge))
            back[...] = jnp.where(low, one, two)
            collect(s)
            return carry

        lax.fori_loop(0, slots, step, 0)

    for k, send in enumerate(sends):
        for m in range(materials):
            send[m] = piece(gradient.at[m], lax.rem(me + k, count), count, half_rows)


def update_kernel(count, maps, power, *refs):
    own, arrived, out = refs[0], refs[1:-1], refs[-1]
    materials, length, _ = maps.shape
    half = length // 2
    me = lax.axis_index("wave")
    half_rows = length // count
    for m in range(materials):
        total = jnp.where(me < count // 2, own[m], arrived[0][m])
        for other in arrived[1:]:
            total = total + other[m]
        here = piece(maps.at[m], lax.rem(me + count // 2, count), count, half_rows)
        out[m] = here + power[...] * total


def join_kernel(count, *refs):
    shares, out = refs[:count], refs[count]
    materials, length, _ = out.shape
    half = length // 2
    me = lax.axis_index("wave")
    half_rows = length // count
    groups = count // 2
    low = lanes(half_rows, length) < half
    for position in range(count):

        @pl.when(me == position)
        def _():
            held = lambda q: shares[(q - position) % count]
            for g in range(groups):
                right, left = held(g), held(g + groups)
                start = g * 2 * half_rows
                for m in range(materials):
                    r, l = right[m], left[m]
                    out[m, start : start + half_rows] = jnp.where(low, l, pltpu.roll(r, half, 1))
                    out[m, start + half_rows : start + 2 * half_rows] = jnp.where(
                        low, pltpu.roll(l, half, 1), r
                    )


def params(mib=40):
    return pltpu.CompilerParams(vmem_limit_bytes=mib * 2**20)


def per_device(tiles, count, maps, measured, offsets, probe, spectrum, wave_index, edge_band, band_coef):
    materials, length, columns = maps.shape
    slots = probe.shape[0]
    half = length // 2
    shape = jax.ShapeDtypeStruct
    half_rows = length // count

    packed = pl.pallas_call(
        pack_kernel,
        out_shape=shape((materials * half + length, length), f32),
        in_specs=[SM, VM, VM],
        out_specs=VM,
        compiler_params=params(),
        name="pack",
    )(offsets, maps, measured)
    halo = lax.ppermute(packed, "tile", [(i, (i - 1) % tiles) for i in range(tiles)])

    table, power = pl.pallas_call(
        lambda *refs: first_kernel(tiles, *refs),
        out_shape=(shape((slots, 3, length, length), bf16), shape((length, length), f32)),
        in_specs=[SM] * 4 + [VM] * 2,
        out_specs=(VM, VM),
        compiler_params=params(),
        cost_estimate=pl.CostEstimate(flops=10**9, bytes_accessed=2**22, transcendentals=0),
        name="tables",
    )(spectrum, wave_index, edge_band, band_coef, maps, probe)

    share = shape((length + half_rows, length), f32)
    psi, far, far_edge, keep, edge_keep, *messages = pl.pallas_call(
        lambda *refs: forward_kernel(tiles, count, *refs),
        out_shape=(
            shape((slots, 2, length, length), f32),
            shape((slots, length, 2 * length), f32),
            shape((slots, length, 2 * length), f32),
            share,
            shape((length, length), f32),
        )
        + (share,) * (count - 1),
        in_specs=[SM] * 3 + [VM] * 5,
        out_specs=(VM,) * (4 + count),
        scratch_shapes=[
            pltpu.VMEM((materials, length, length), f32),
            pltpu.VMEM((length, length), f32),
            pltpu.VMEM((length, length), f32),
        ],
        compiler_params=params(),
        name="forward",
    )(spectrum, edge_band, band_coef, maps, halo, probe, table, power)

    both = ("tile", "wave")
    shares, edges = [keep], [edge_keep]
    for k in range(1, count):
        ring = [(w, (w + k) % count) for w in range(count)]
        shares.append(lax.ppermute(messages[k - 1], "wave", ring))
        last = (tiles - 1) * count
        edges.append(lax.ppermute(edge_keep, both, [(last + a, last + b) for a, b in ring]))

    *sends, scale = pl.pallas_call(
        lambda *refs: backward_kernel(tiles, count, *refs),
        out_shape=(shape((materials, half_rows, length), f32),) * count
        + (shape((half_rows, length), f32),),
        in_specs=[SM] * 4 + [VM] * (6 + 2 * count),
        out_specs=(VM,) * (count + 1),
        scratch_shapes=[
            pltpu.VMEM((length, length), f32),
            pltpu.VMEM((length, length), f32),
            pltpu.VMEM((materials, length, length), f32),
            pltpu.VMEM((length, 2 * length), f32),
        ],
        compiler_params=params(),
        name="backward",
    )(offsets, spectrum, edge_band, band_coef, measured, halo, table, psi, far, far_edge, *shares, *edges)

    def owner(t, q):
        return (t + (q >= count // 2)) % tiles * count + q

    arrived = []
    for k in range(count):
        pairs = [
            (t * count + w, owner(t, (w + k) % count)) for t in range(tiles) for w in range(count)
        ]
        arrived.append(lax.ppermute(sends[k], both, [p for p in pairs if p[0] != p[1]]))

    new = pl.pallas_call(
        lambda *refs: update_kernel(count, *refs),
        out_shape=shape((materials, half_rows, length), f32),
        in_specs=[VM] * (3 + count),
        out_specs=VM,
        compiler_params=params(),
        name="update",
    )(maps, scale, sends[0], *arrived)

    parts = [new]
    for k in range(1, count):
        parts.append(lax.ppermute(new, "wave", [((w + k) % count, w) for w in range(count)]))
    return pl.pallas_call(
        lambda *refs: join_kernel(count, *refs),
        out_shape=shape((materials, length, length), f32),
        in_specs=[VM] * count,
        out_specs=VM,
        compiler_params=params(),
        name="join",
    )(*parts)


def solution(mesh):
    in_specs = (
        P(None, None, "tile"),
        P("tile", None, None),
        P("tile"),
        P("wave", None, None, None),
        P("wave"),
        P("wave"),
        P("wave", None),
        P(),
    )
    out_specs = P(None, None, "tile")
    tiles, count = mesh.shape["tile"], mesh.shape["wave"]
    return jax.shard_map(
        lambda *args: per_device(tiles, count, *args),
        mesh=mesh,
        in_specs=in_specs,
        out_specs=out_specs,
        check_vma=False,
    )
```

```python
import math

import jax
import jax.numpy as jnp
import numpy as np
from jax import lax
from jax.experimental import pallas as pl
from jax.experimental.pallas import tpu as pltpu
from jax.sharding import PartitionSpec as P

WAVES = 48

relax = 4.0
floor_level = 1.0

UNROLL = 4
EDGE_UNROLL = 2

VM = pl.BlockSpec(memory_space=pltpu.VMEM)
ANY = pl.BlockSpec(memory_space=pltpu.HBM)
f32 = jnp.float32
bf16 = jnp.bfloat16


def fit(parity, degree):
    nodes = 0.5 * np.cos(np.pi * (np.arange(400) + 0.5) / 800)
    turns = 2 * np.pi * nodes
    value = np.sin(turns) if parity else np.cos(turns)
    powers = np.stack([nodes ** (parity + 2 * i) for i in range(degree)], axis=1)
    return [float(c) for c in np.linalg.lstsq(powers, value, rcond=None)[0]]


SIN = fit(1, 6)
COS = fit(0, 7)


def horner(square, coefs):
    total = coefs[-1]
    for c in coefs[-2::-1]:
        total = total * square + c
    return total


def cos_sin(turns):
    r = turns - jnp.round(turns)
    square = r * r
    return horner(square, COS), horner(square, SIN) * r


def lanes(rows, length):
    return lax.broadcasted_iota(jnp.int32, (rows, length), 1)


def halves_packed(top, bottom, upper):
    length = top.shape[-1]
    half = length // 2
    low = lanes(top.shape[0], length) < half
    if upper:
        return jnp.where(low, pltpu.roll(top, half, 1), bottom)
    return jnp.where(low, top, pltpu.roll(bottom, half, 1))


def block(table_ref, s, kind):
    re, im, neg = table_ref[s, 0], table_ref[s, 1], table_ref[s, 2]
    top, bottom = ((re, neg), (im, re)) if kind == "L" else ((re, im), (neg, re))
    return jnp.concatenate(
        [jnp.concatenate(top, axis=1), jnp.concatenate(bottom, axis=1)], axis=0
    )


def pack_kernel(offsets_any, maps_any, measured_any, out, right_root, offsets, maps, measured, sems):
    copies = [
        pltpu.make_async_copy(source, target, sems.at[i])
        for i, (source, target) in enumerate(
            ((offsets_any, offsets), (maps_any, maps), (measured_any, measured))
        )
    ]
    for copy in copies:
        copy.start()
    materials, length, _ = maps.shape
    half = length // 2
    copies[1].wait()
    for m in range(materials):
        out[m * half : (m + 1) * half] = halves_packed(maps[m, :half], maps[m, half:], False)
    copies[0].wait()
    copies[2].wait()
    left_first = offsets[0] < offsets[1]
    first, second = jnp.sqrt(measured[0]), jnp.sqrt(measured[1])
    out[materials * half :] = jnp.where(left_first, first, second)
    right_root[...] = jnp.where(left_first, second, first)


def piece(array, q, count, half_rows):
    groups = count // 2
    rows = 2 * half_rows
    start = pl.multiple_of(lax.rem(q, groups) * rows, half_rows)
    top = array[pl.ds(start, half_rows), :]
    bottom = array[pl.ds(start + half_rows, half_rows), :]
    return jnp.where(
        q < groups, halves_packed(top, bottom, False), halves_packed(top, bottom, True)
    )


def first_kernel(
    tiles, count, spectrum_any, wave_any, edge_any, band_any, maps_any, probe_any,
    table, coef, probe, own, here, power,
    spectrum, wave_index, edge_band, band_coef, maps, sems,
):
    copies = [
        pltpu.make_async_copy(source, target, sems.at[i])
        for i, (source, target) in enumerate(
            (
                (wave_any, wave_index),
                (edge_any, edge_band),
                (band_any, band_coef),
                (spectrum_any, spectrum),
                (maps_any, maps),
                (probe_any, probe),
            )
        )
    ]
    for copy in copies:
        copy.start()
    materials, length, _ = maps.shape
    half = length // 2
    slots = probe.shape[0]
    tile = lax.axis_index("tile")
    me = lax.axis_index("wave")
    group = 8
    centred_lane = (lanes(group, length) - half).astype(f32)
    row = lax.broadcasted_iota(jnp.int32, (group, length), 0)
    fine = row.astype(f32) * centred_lane / length
    normaliser = 1.0 / math.sqrt(length)
    coarse_rows = length // group
    copies[0].wait()

    def tables(s, carry):
        which = jnp.full((group, length), wave_index[s], jnp.int32).astype(f32)
        sampling = 0.6 + 0.4 * which / (WAVES - 1)
        fine_cos, fine_sin = cos_sin(sampling * fine)
        fine_cos, fine_sin = fine_cos * normaliser, fine_sin * normaliser
        for base in range(0, coarse_rows, group):
            step = ((row + base) * group - half).astype(f32) * centred_lane / length
            cos, sin = cos_sin(sampling * step)
            for i in range(0, group, 2):
                parts = []
                for j in (i, i + 1):
                    c = jnp.broadcast_to(cos[j : j + 1], (group, length))
                    n = jnp.broadcast_to(sin[j : j + 1], (group, length))
                    parts.append((c * fine_cos - n * fine_sin, n * fine_cos + c * fine_sin))
                at = pl.ds((base + i) * group, 2 * group)
                re = jnp.concatenate([parts[0][0], parts[1][0]], axis=0).astype(bf16)
                positive = jnp.concatenate([parts[0][1], parts[1][1]], axis=0)
                table[s, 0, at, :] = re
                table[s, 1, at, :] = (-positive).astype(bf16)
                table[s, 2, at, :] = positive.astype(bf16)
        return carry

    lax.fori_loop(0, slots, tables, 0, unroll=2)

    for copy in copies[1:]:
        copy.wait()
    for s in range(slots):
        for m in range(materials):
            band = edge_band[m, s]
            a, b = band_coef[band, 0, m], band_coef[band, 1, m]
            coef[s, m, :] = jnp.full((length,), a * (-math.log2(math.e)), f32)
            coef[s, materials + m, :] = jnp.full((length,), b * (0.5 / math.pi), f32)
            coef[s, 2 * materials + m, :] = jnp.full((length,), a, f32)
            coef[s, 3 * materials + m, :] = jnp.full((length,), b, f32)
        coef[s, 4 * materials, :] = jnp.full((length,), spectrum[s], f32)
    for m in range(materials):
        own[m] = pltpu.roll(maps[m], half, 1)
    chunk = 32
    low = lanes(chunk, length) < half
    frames = jnp.where(
        low,
        jnp.where(tile == tiles - 1, 1.0, 2.0),
        jnp.where(tile == 0, 1.0, 2.0),
    )
    for start in range(0, length, chunk):
        at = slice(start, start + chunk)
        window = [own[m, at] for m in range(materials)]

        def add(s, total):
            absorb = None
            for m in range(materials):
                term = coef[s, m : m + 1] * window[m]
                absorb = term if absorb is None else absorb + term
            re, im = probe[s, 0, at], probe[s, 1, at]
            weight = coef[s, 4 * materials : 4 * materials + 1]
            return total + (weight * jnp.exp2(absorb + absorb)) * (re * re + im * im)

        total = lax.fori_loop(0, slots, add, jnp.zeros((chunk, length), f32), unroll=4)
        power[at] = frames * total
    half_rows = length // count
    for m in range(materials):
        here[m] = piece(own.at[m], me, count, half_rows)


CHUNK = 32


def transform(left, right, fields):
    length = fields[0][0].shape[0]
    stacked = jnp.concatenate(
        [jnp.concatenate([re.astype(bf16), im.astype(bf16)], axis=0) for re, im in fields], axis=1
    )
    mid = jnp.dot(left, stacked, preferred_element_type=f32).astype(bf16)
    beside = jnp.concatenate(
        [
            jnp.concatenate(
                [mid[:length, i * length : (i + 1) * length], mid[length:, i * length : (i + 1) * length]], axis=1
            )
            for i in range(len(fields))
        ],
        axis=0,
    )
    return jnp.dot(beside, right, preferred_element_type=f32)


def forward_kernel(
    tiles, count, own, halo, probe, table, coef, power,
    psi, far, *messages_and_scratch,
):
    messages = messages_and_scratch[:count]
    window, total = messages_and_scratch[count:]
    materials, length, _ = own.shape
    half = length // 2
    slots = probe.shape[0]
    edge = lax.axis_index("tile") == tiles - 1
    me = lax.axis_index("wave")
    low = lanes(half, length) < half
    for m in range(materials):
        packed = halo[m * half : (m + 1) * half]
        window[m, :half] = jnp.where(low, own[m, :half], pltpu.roll(packed, half, 1))
        window[m, half:] = jnp.where(low, own[m, half:], packed)
    total[...] = jnp.zeros_like(total)

    def exit_wave(s):
        for start in range(0, length, CHUNK):
            at = slice(start, start + CHUNK)
            absorb, phase = None, None
            for m in range(materials):
                w = window[m, at]
                a = coef[s, m : m + 1] * w
                b = coef[s, materials + m : materials + m + 1] * w
                absorb = a if absorb is None else absorb + a
                phase = b if phase is None else phase + b
            damping = jnp.exp2(absorb)
            cos, sin = cos_sin(phase)
            cos, sin = damping * cos, damping * sin
            re, im = probe[s, 0, at], probe[s, 1, at]
            psi[s, 0, at] = re * cos - im * sin
            psi[s, 1, at] = re * sin + im * cos

    def add_intensity(s, got, at):
        re, im = got[:, :length], got[:, length:]
        total[at : at + length] += coef[s, 4 * materials : 4 * materials + 1] * (re * re + im * im)

    @pl.when(jnp.logical_not(edge))
    def _():
        def step(s, carry):
            exit_wave(s)
            got = transform(block(table, s, "L"), block(table, s, "R"), [(psi[s, 0], psi[s, 1])])
            far[s, :length] = got
            add_intensity(s, got, 0)
            return carry

        lax.fori_loop(0, slots, step, 0, unroll=UNROLL)

    @pl.when(edge)
    def _():
        low = lanes(length, length) < half

        def step(s, carry):
            exit_wave(s)
            re, im, bare_re, bare_im = psi[s, 0], psi[s, 1], probe[s, 0], probe[s, 1]
            got = transform(
                block(table, s, "L"),
                block(table, s, "R"),
                [
                    (jnp.where(low, re, bare_re), jnp.where(low, im, bare_im)),
                    (jnp.where(low, bare_re, re), jnp.where(low, bare_im, im)),
                ],
            )
            far[s] = got
            add_intensity(s, got[:length], 0)
            add_intensity(s, got[length:], length)
            return carry

        lax.fori_loop(0, slots, step, 0, unroll=EDGE_UNROLL)

    half_rows = length // count
    for k, message in enumerate(messages):
        message[: 2 * length] = total[...]
        message[2 * length :] = piece(power, jnp.bitwise_xor(me, k), count, half_rows)


def backward_kernel(tiles, count, right_root, halo, table, coef, psi, far, *rest):
    shares, rest = rest[:count], rest[count:]
    sends, rest = rest[:count], rest[count:]
    scale, shortfall, gradient, back = rest
    length = right_root.shape[0]
    materials = gradient.shape[0]
    half = length // 2
    slots = psi.shape[0]
    edge = lax.axis_index("tile") == tiles - 1
    me = lax.axis_index("wave")
    half_rows = length // count
    powers = shares[0][2 * length :]
    for share in shares[1:]:
        powers = powers + share[2 * length :]
    scale[...] = relax / (powers + 1.0)
    gradient[...] = jnp.zeros_like(gradient)

    def inverse(at):
        intensity = shares[0][at : at + length]
        for share in shares[1:]:
            intensity = intensity + share[at : at + length]
        return lax.rsqrt(jnp.maximum(intensity, floor_level))

    left_root = halo.at[materials * half :]

    def delta(s, at):
        factor = coef[s, 4 * materials : 4 * materials + 1] * shortfall[at : at + length]
        return factor * far[s, at : at + length, :length], factor * far[s, at : at + length, length:]

    def collect(s):
        for start in range(0, length, CHUNK):
            at = slice(start, start + CHUNK)
            re, im = psi[s, 0, at], psi[s, 1, at]
            back_re, back_im = back[at, :length], back[at, length:]
            cross_re = re * back_re + im * back_im
            cross_im = re * back_im - im * back_re
            for m in range(materials):
                a = coef[s, 2 * materials + m : 2 * materials + m + 1]
                b = coef[s, 3 * materials + m : 3 * materials + m + 1]
                gradient[m, at] += b * cross_im - a * cross_re

    @pl.when(jnp.logical_not(edge))
    def _():
        shortfall[:length] = (right_root[...] + left_root[...]) * inverse(0) - 2.0

        def step(s, carry):
            back[...] = transform(block(table, s, "R"), block(table, s, "L"), [delta(s, 0)])
            collect(s)
            return carry

        lax.fori_loop(0, slots, step, 0, unroll=UNROLL)

    @pl.when(edge)
    def _():
        shortfall[:length] = right_root[...] * inverse(0) - 1.0
        shortfall[length:] = left_root[...] * inverse(length) - 1.0
        low = (lax.broadcasted_iota(jnp.int32, (length, 2 * length), 1) & (length - 1)) < half

        def step(s, carry):
            both = transform(
                block(table, s, "R"), block(table, s, "L"), [delta(s, 0), delta(s, length)]
            )
            back[...] = jnp.where(low, both[:length], both[length:])
            collect(s)
            return carry

        lax.fori_loop(0, slots, step, 0, unroll=EDGE_UNROLL)

    for k, send in enumerate(sends):
        for m in range(materials):
            send[m] = piece(gradient.at[m], jnp.bitwise_xor(me, k), count, half_rows)


def update_kernel(count, here, scale, *refs):
    own, arrived, out = refs[0], refs[1:-1], refs[-1]
    me = lax.axis_index("wave")
    for m in range(here.shape[0]):
        total = jnp.where(me < count // 2, own[m], arrived[0][m])
        for other in arrived[1:]:
            total = total + other[m]
        out[m] = here[m] + scale[...] * total


def join_kernel(count, *refs):
    shares, out = refs[:count], refs[count]
    materials, length, _ = out.shape
    half = length // 2
    me = lax.axis_index("wave")
    half_rows = length // count
    groups = count // 2
    low = lanes(half_rows, length) < half
    for position in range(count):

        @pl.when(me == position)
        def _():
            held = lambda q: shares[q ^ position]
            for g in range(groups):
                right, left = held(g), held(g + groups)
                start = g * 2 * half_rows
                for m in range(materials):
                    r, l = right[m], left[m]
                    out[m, start : start + half_rows] = jnp.where(low, l, pltpu.roll(r, half, 1))
                    out[m, start + half_rows : start + 2 * half_rows] = jnp.where(
                        low, pltpu.roll(l, half, 1), r
                    )


def in_hbm(array):
    return pltpu.with_memory_space_constraint(array, pltpu.HBM)


def params(mib=40):
    return pltpu.CompilerParams(vmem_limit_bytes=mib * 2**20)


def per_device(tiles, count, maps, measured, offsets, probe, spectrum, wave_index, edge_band, band_coef):
    materials, length, columns = maps.shape
    slots = probe.shape[0]
    half = length // 2
    shape = jax.ShapeDtypeStruct
    half_rows = length // count
    square = shape((length, length), f32)
    share = shape((materials, half_rows, length), f32)

    packed, right_root = pl.pallas_call(
        pack_kernel,
        out_shape=(shape((materials * half + length, length), f32), square),
        in_specs=[ANY] * 3,
        out_specs=(VM, VM),
        scratch_shapes=[
            pltpu.SMEM(offsets.shape, jnp.int32),
            pltpu.VMEM(maps.shape, f32),
            pltpu.VMEM(measured.shape, f32),
            pltpu.SemaphoreType.DMA((3,)),
        ],
        compiler_params=params(),
        name="pack",
    )(*map(in_hbm, (offsets, maps, measured)))
    halo = lax.ppermute(packed, "tile", [(i, (i - 1) % tiles) for i in range(tiles)])

    band_first = jnp.transpose(band_coef, (1, 0, 2))
    table, coef, near_probe, own, here, power = pl.pallas_call(
        lambda *refs: first_kernel(tiles, count, *refs),
        out_shape=(
            shape((slots, 3, length, length), bf16),
            shape((slots, 6 * materials, length), f32),
            shape(probe.shape, f32),
            shape(maps.shape, f32),
            share,
            square,
        ),
        in_specs=[ANY] * 6,
        out_specs=(VM,) * 6,
        scratch_shapes=[
            pltpu.SMEM(spectrum.shape, f32),
            pltpu.SMEM(wave_index.shape, jnp.int32),
            pltpu.SMEM(edge_band.shape[::-1], jnp.int32),
            pltpu.SMEM(band_first.shape, f32),
            pltpu.VMEM(maps.shape, f32),
            pltpu.SemaphoreType.DMA((6,)),
        ],
        compiler_params=params(),
        cost_estimate=pl.CostEstimate(flops=10**9, bytes_accessed=2**22, transcendentals=0),
        name="tables",
    )(*map(in_hbm, (spectrum, wave_index, edge_band.T, band_first, maps, probe)))

    message = shape((2 * length + half_rows, length), f32)
    psi, far, *messages = pl.pallas_call(
        lambda *refs: forward_kernel(tiles, count, *refs),
        out_shape=(
            shape((slots, 2, length, length), f32),
            shape((slots, 2 * length, 2 * length), f32),
        )
        + (message,) * count,
        in_specs=[VM] * 6,
        out_specs=(VM,) * (2 + count),
        scratch_shapes=[
            pltpu.VMEM((materials, length, length), f32),
            pltpu.VMEM((2 * length, length), f32),
        ],
        compiler_params=params(),
        name="forward",
    )(own, halo, near_probe, table, coef, power)

    shares = [messages[0]]
    for k in range(1, count):
        shares.append(lax.ppermute(messages[k], "wave", [(w, w ^ k) for w in range(count)]))

    *sends, scale = pl.pallas_call(
        lambda *refs: backward_kernel(tiles, count, *refs),
        out_shape=(share,) * count + (shape((half_rows, length), f32),),
        in_specs=[VM] * (6 + count),
        out_specs=(VM,) * (count + 1),
        scratch_shapes=[
            pltpu.VMEM((2 * length, length), f32),
            pltpu.VMEM((materials, length, length), f32),
            pltpu.VMEM((length, 2 * length), f32),
        ],
        compiler_params=params(),
        name="backward",
    )(right_root, halo, table, coef, psi, far, *shares)

    def owner(t, q):
        return (t + (q >= count // 2)) % tiles * count + q

    arrived = []
    for k in range(count):
        pairs = [(t * count + w, owner(t, w ^ k)) for t in range(tiles) for w in range(count)]
        arrived.append(lax.ppermute(sends[k], ("tile", "wave"), [p for p in pairs if p[0] != p[1]]))

    new = pl.pallas_call(
        lambda *refs: update_kernel(count, *refs),
        out_shape=share,
        in_specs=[VM] * (3 + count),
        out_specs=VM,
        compiler_params=params(),
        name="update",
    )(here, scale, sends[0], *arrived)

    parts = [new]
    for k in range(1, count):
        parts.append(lax.ppermute(new, "wave", [(w, w ^ k) for w in range(count)]))
    return pl.pallas_call(
        lambda *refs: join_kernel(count, *refs),
        out_shape=shape((materials, length, length), f32),
        in_specs=[VM] * count,
        out_specs=VM,
        compiler_params=params(),
        name="join",
    )(*parts)


def solution(mesh):
    in_specs = (
        P(None, None, "tile"),
        P("tile", None, None),
        P("tile"),
        P("wave", None, None, None),
        P("wave"),
        P("wave"),
        P("wave", None),
        P(),
    )
    out_specs = P(None, None, "tile")
    tiles, count = mesh.shape["tile"], mesh.shape["wave"]
    return jax.shard_map(
        lambda *args: per_device(tiles, count, *args),
        mesh=mesh,
        in_specs=in_specs,
        out_specs=out_specs,
        check_vma=False,
    )
```

```python
import math

import jax
import jax.numpy as jnp
import numpy as np
from jax import lax
from jax.experimental import pallas as pl
from jax.experimental.pallas import tpu as pltpu
from jax.sharding import PartitionSpec as P

WAVES = 48

relax = 4.0
floor_level = 1.0

UNROLL = 12
EDGE_UNROLL = 4
CHUNK = 32

VM = pl.BlockSpec(memory_space=pltpu.VMEM)
ANY = pl.BlockSpec(memory_space=pltpu.HBM)
f32 = jnp.float32
bf16 = jnp.bfloat16


def fit(parity, degree):
    nodes = 0.5 * np.cos(np.pi * (np.arange(400) + 0.5) / 800)
    turns = 2 * np.pi * nodes
    value = np.sin(turns) if parity else np.cos(turns)
    powers = np.stack([nodes ** (parity + 2 * i) for i in range(degree)], axis=1)
    return [float(c) for c in np.linalg.lstsq(powers, value, rcond=None)[0]]


SIN = fit(1, 6)
COS = fit(0, 7)


def horner(square, coefs):
    total = coefs[-1]
    for c in coefs[-2::-1]:
        total = total * square + c
    return total


def cos_sin(turns):
    r = turns - jnp.round(turns)
    square = r * r
    return horner(square, COS), horner(square, SIN) * r


def lanes(rows, length):
    return lax.broadcasted_iota(jnp.int32, (rows, length), 1)


def halves_packed(top, bottom, upper):
    length = top.shape[-1]
    half = length // 2
    low = lanes(top.shape[0], length) < half
    if upper:
        return jnp.where(low, pltpu.roll(top, half, 1), bottom)
    return jnp.where(low, top, pltpu.roll(bottom, half, 1))


def block(table_ref, s, kind):
    re, im, neg = table_ref[s, 0], table_ref[s, 1], table_ref[s, 2]
    top, bottom = ((re, neg), (im, re)) if kind == "L" else ((re, im), (neg, re))
    return jnp.concatenate(
        [jnp.concatenate(top, axis=1), jnp.concatenate(bottom, axis=1)], axis=0
    )


def piece(array, q, count, half_rows):
    groups = count // 2
    rows = 2 * half_rows
    start = pl.multiple_of(lax.rem(q, groups) * rows, half_rows)
    top = array[pl.ds(start, half_rows), :]
    bottom = array[pl.ds(start + half_rows, half_rows), :]
    return jnp.where(
        q < groups, halves_packed(top, bottom, False), halves_packed(top, bottom, True)
    )


def first_kernel(
    spectrum_any, wave_any, edge_any, band_any, maps_any, probe_any,
    table, coef, probe, near, own, far_edge, total_edge,
    spectrum, wave_index, edge_band, band_coef, maps, packed, sems,
):
    copies = [
        pltpu.make_async_copy(source, target, sems.at[i])
        for i, (source, target) in enumerate(
            (
                (wave_any, wave_index),
                (edge_any, edge_band),
                (band_any, band_coef),
                (spectrum_any, spectrum),
                (maps_any, maps),
                (probe_any, probe),
            )
        )
    ]
    for copy in copies:
        copy.start()
    materials, length, _ = maps.shape
    half = length // 2
    slots = probe.shape[0]
    group = 8
    centred_lane = (lanes(group, length) - half).astype(f32)
    row = lax.broadcasted_iota(jnp.int32, (group, length), 0)
    fine = row.astype(f32) * centred_lane / length
    normaliser = 1.0 / math.sqrt(length)
    coarse_rows = length // group
    copies[0].wait()

    def tables(s, carry):
        which = jnp.full((group, length), wave_index[s], jnp.int32).astype(f32)
        sampling = 0.6 + 0.4 * which / (WAVES - 1)
        fine_cos, fine_sin = cos_sin(sampling * fine)
        fine_cos, fine_sin = fine_cos * normaliser, fine_sin * normaliser
        for base in range(0, coarse_rows, group):
            step = ((row + base) * group - half).astype(f32) * centred_lane / length
            cos, sin = cos_sin(sampling * step)
            for i in range(0, group, 2):
                parts = []
                for j in (i, i + 1):
                    c = jnp.broadcast_to(cos[j : j + 1], (group, length))
                    n = jnp.broadcast_to(sin[j : j + 1], (group, length))
                    parts.append((c * fine_cos - n * fine_sin, n * fine_cos + c * fine_sin))
                at = pl.ds((base + i) * group, 2 * group)
                re = jnp.concatenate([parts[0][0], parts[1][0]], axis=0).astype(bf16)
                positive = jnp.concatenate([parts[0][1], parts[1][1]], axis=0)
                table[s, 0, at, :] = re
                table[s, 1, at, :] = (-positive).astype(bf16)
                table[s, 2, at, :] = positive.astype(bf16)
        return carry

    lax.fori_loop(0, slots, tables, 0, unroll=2)

    for copy in copies[1:]:
        copy.wait()
    for s in range(slots):
        for m in range(materials):
            band = edge_band[m, s]
            a, b = band_coef[band, 0, m], band_coef[band, 1, m]
            coef[s, m, :] = jnp.full((length,), a * (-math.log2(math.e)), f32)
            coef[s, materials + m, :] = jnp.full((length,), b * (0.5 / math.pi), f32)
            coef[s, 2 * materials + m, :] = jnp.full((length,), a, f32)
            coef[s, 3 * materials + m, :] = jnp.full((length,), b, f32)
        coef[s, 4 * materials, :] = jnp.full((length,), spectrum[s], f32)
    for m in range(materials):
        own[m] = pltpu.roll(maps[m], half, 1)
        packed[m] = halves_packed(own[m, :half], own[m, half:], False)

    def near_object(s, carry):
        for start in range(0, half, CHUNK):
            parts = object_of(coef, s, [packed[m, start : start + CHUNK] for m in range(materials)])
            for i, part in enumerate(parts):
                near[s, i, start : start + CHUNK] = part
                near[s, i, half + start : half + start + CHUNK] = pltpu.roll(part, half, 1)
        return carry

    lax.fori_loop(0, slots, near_object, 0, unroll=2)

    @pl.when(lax.axis_index("tile") == lax.axis_size("tile") - 1)
    def _():
        total_edge[...] = jnp.zeros_like(total_edge)
        low = lanes(length, length) < half

        def step(s, carry):
            re, im, cos, sin = probe[s, 0], probe[s, 1], near[s, 0], near[s, 1]
            field = [
                (jnp.where(low, re * cos - im * sin, re), jnp.where(low, re * sin + im * cos, im))
            ]
            got = transform(block(table, s, "L"), block(table, s, "R"), field)
            far_edge[s] = got
            re, im = got[:, :length], got[:, length:]
            total_edge[...] += coef[s, 4 * materials : 4 * materials + 1] * (re * re + im * im)
            return carry

        lax.fori_loop(0, slots, step, 0, unroll=EDGE_UNROLL)


def power_kernel(
    count, offsets_any, measured_any, coef, probe, own,
    here, power, left_root, right_root,
    offsets, measured, sems,
):
    copies = [
        pltpu.make_async_copy(source, target, sems.at[i])
        for i, (source, target) in enumerate(((offsets_any, offsets), (measured_any, measured)))
    ]
    for copy in copies:
        copy.start()
    materials, length, _ = own.shape
    half = length // 2
    slots = probe.shape[0]
    tile, tiles = lax.axis_index("tile"), lax.axis_size("tile")
    me = lax.axis_index("wave")
    low = lanes(CHUNK, length) < half
    frames = jnp.where(
        low,
        jnp.where(tile == tiles - 1, 1.0, 2.0),
        jnp.where(tile == 0, 1.0, 2.0),
    )
    for start in range(0, length, CHUNK):
        at = slice(start, start + CHUNK)
        window = [own[m, at] for m in range(materials)]

        def add(s, total):
            absorb = None
            for m in range(materials):
                term = coef[s, m : m + 1] * window[m]
                absorb = term if absorb is None else absorb + term
            re, im = probe[s, 0, at], probe[s, 1, at]
            weight = coef[s, 4 * materials : 4 * materials + 1]
            return total + (weight * jnp.exp2(absorb + absorb)) * (re * re + im * im)

        total = lax.fori_loop(0, slots, add, jnp.zeros((CHUNK, length), f32), unroll=4)
        power[at] = frames * total
    half_rows = length // count
    for m in range(materials):
        here[m] = piece(own.at[m], me, count, half_rows)
    for copy in copies:
        copy.wait()
    left_first = offsets[0] < offsets[1]
    first, second = jnp.sqrt(measured[0]), jnp.sqrt(measured[1])
    left_root[...] = jnp.where(left_first, first, second)
    right_root[...] = jnp.where(left_first, second, first)


def object_of(coef, s, window):
    materials = len(window)
    absorb, phase = None, None
    for m, w in enumerate(window):
        a = coef[s, m : m + 1] * w
        b = coef[s, materials + m : materials + m + 1] * w
        absorb = a if absorb is None else absorb + a
        phase = b if phase is None else phase + b
    damping = jnp.exp2(absorb)
    cos, sin = cos_sin(phase)
    return damping * cos, damping * sin


def transform(left, right, fields):
    length = fields[0][0].shape[0]
    stacked = jnp.concatenate(
        [jnp.concatenate([re.astype(bf16), im.astype(bf16)], axis=0) for re, im in fields], axis=1
    )
    mid = jnp.dot(left, stacked, preferred_element_type=f32).astype(bf16)
    beside = jnp.concatenate(
        [
            jnp.concatenate(
                [mid[:length, i * length : (i + 1) * length], mid[length:, i * length : (i + 1) * length]], axis=1
            )
            for i in range(len(fields))
        ],
        axis=0,
    )
    return jnp.dot(beside, right, preferred_element_type=f32)


def forward_kernel(count, near, halo, probe, table, coef, power, psi, far, *rest):
    messages, (beyond, total) = rest[:count], rest[count:]
    materials, length, _ = halo.shape
    half = length // 2
    slots = probe.shape[0]
    me = lax.axis_index("wave")
    for m in range(materials):
        beyond[m] = halves_packed(halo[m, :half], halo[m, half:], False)
    total[...] = jnp.zeros_like(total)
    low = lanes(CHUNK, length) < half

    def exit_wave(s):
        for start in range(0, half, CHUNK):
            parts = object_of(coef, s, [beyond[m, start : start + CHUNK] for m in range(materials)])
            upper, lower = slice(start, start + CHUNK), slice(half + start, half + start + CHUNK)
            for at, turned in ((upper, True), (lower, False)):
                cos, sin = [
                    jnp.where(low, near[s, i, at], pltpu.roll(part, half, 1) if turned else part)
                    for i, part in enumerate(parts)
                ]
                re, im = probe[s, 0, at], probe[s, 1, at]
                psi[s, 0, at] = re * cos - im * sin
                psi[s, 1, at] = re * sin + im * cos

    def step(s, joined):
        exit_wave(s)
        re, im = psi[s, 0], psi[s, 1]
        if joined:
            low = lanes(length, length) < half
            re, im = jnp.where(low, probe[s, 0], re), jnp.where(low, probe[s, 1], im)
        got = transform(block(table, s, "L"), block(table, s, "R"), [(re, im)])
        far[s] = got
        re, im = got[:, :length], got[:, length:]
        total[...] += coef[s, 4 * materials : 4 * materials + 1] * (re * re + im * im)

    edge = lax.axis_index("tile") == lax.axis_size("tile") - 1
    for joined in (False, True):

        @pl.when(edge == joined)
        def _():
            lax.fori_loop(
                0, slots, lambda s, c: (step(s, joined), c)[1], 0, unroll=EDGE_UNROLL if joined else UNROLL
            )

    half_rows = length // count
    for k, message in enumerate(messages):
        message[:length] = total[...]
        message[length:] = piece(power, jnp.bitwise_xor(me, k), count, half_rows)


def backward_kernel(tiles, count, right_root, left_root, table, coef, psi, far, far_edge, *rest):
    shares, rest = rest[:count], rest[count:]
    edges, rest = rest[:count], rest[count:]
    sends, rest = rest[:count], rest[count:]
    scale, shortfall, gradient, back = rest
    length = right_root.shape[0]
    materials = gradient.shape[0]
    half = length // 2
    slots = psi.shape[0]
    edge = lax.axis_index("tile") == tiles - 1
    me = lax.axis_index("wave")
    half_rows = length // count
    powers = shares[0][length:]
    for share in shares[1:]:
        powers = powers + share[length:]
    scale[...] = relax / (powers + 1.0)
    gradient[...] = jnp.zeros_like(gradient)

    def inverse(shares):
        intensity = shares[0][:length]
        for share in shares[1:]:
            intensity = intensity + share[:length]
        return lax.rsqrt(jnp.maximum(intensity, floor_level))

    def delta(s, far, at):
        factor = coef[s, 4 * materials : 4 * materials + 1] * shortfall[at : at + length]
        return factor * far[s, :, :length], factor * far[s, :, length:]

    def collect(s):
        for start in range(0, length, CHUNK):
            at = slice(start, start + CHUNK)
            re, im = psi[s, 0, at], psi[s, 1, at]
            back_re, back_im = back[at, :length], back[at, length:]
            cross_re = re * back_re + im * back_im
            cross_im = re * back_im - im * back_re
            for m in range(materials):
                a = coef[s, 2 * materials + m : 2 * materials + m + 1]
                b = coef[s, 3 * materials + m : 3 * materials + m + 1]
                gradient[m, at] += b * cross_im - a * cross_re

    @pl.when(jnp.logical_not(edge))
    def _():
        shortfall[:length] = (right_root[...] + left_root[...]) * inverse(shares) - 2.0

        def step(s, carry):
            back[...] = transform(block(table, s, "R"), block(table, s, "L"), [delta(s, far, 0)])
            collect(s)
            return carry

        lax.fori_loop(0, slots, step, 0, unroll=UNROLL)

    @pl.when(edge)
    def _():
        shortfall[:length] = left_root[...] * inverse(shares) - 1.0
        shortfall[length:] = right_root[...] * inverse(edges) - 1.0
        low = (lax.broadcasted_iota(jnp.int32, (length, 2 * length), 1) & (length - 1)) < half

        def step(s, carry):
            both = transform(
                block(table, s, "R"), block(table, s, "L"), [delta(s, far, 0), delta(s, far_edge, length)]
            )
            back[...] = jnp.where(low, both[length:], both[:length])
            collect(s)
            return carry

        lax.fori_loop(0, slots, step, 0, unroll=EDGE_UNROLL)

    for k, send in enumerate(sends):
        for m in range(materials):
            send[m] = piece(gradient.at[m], jnp.bitwise_xor(me, k), count, half_rows)


def update_kernel(count, here, scale, *refs):
    own, arrived, out = refs[0], refs[1:-1], refs[-1]
    me = lax.axis_index("wave")
    for m in range(here.shape[0]):
        total = jnp.where(me < count // 2, own[m], arrived[0][m])
        for other in arrived[1:]:
            total = total + other[m]
        out[m] = here[m] + scale[...] * total


def join_kernel(count, *refs):
    shares, out = refs[:count], refs[count]
    materials, length, _ = out.shape
    half = length // 2
    me = lax.axis_index("wave")
    half_rows = length // count
    groups = count // 2
    low = lanes(half_rows, length) < half
    for position in range(count):

        @pl.when(me == position)
        def _():
            held = lambda q: shares[q ^ position]
            for g in range(groups):
                right, left = held(g), held(g + groups)
                start = g * 2 * half_rows
                for m in range(materials):
                    r, l = right[m], left[m]
                    out[m, start : start + half_rows] = jnp.where(low, l, pltpu.roll(r, half, 1))
                    out[m, start + half_rows : start + 2 * half_rows] = jnp.where(
                        low, pltpu.roll(l, half, 1), r
                    )


def in_hbm(array):
    return pltpu.with_memory_space_constraint(array, pltpu.HBM)


def params(mib=40):
    return pltpu.CompilerParams(vmem_limit_bytes=mib * 2**20)


def per_device(tiles, count, maps, measured, offsets, probe, spectrum, wave_index, edge_band, band_coef):
    materials, length, columns = maps.shape
    slots = probe.shape[0]
    half = length // 2
    shape = jax.ShapeDtypeStruct
    half_rows = length // count
    square = shape((length, length), f32)
    share = shape((materials, half_rows, length), f32)

    ring = [(i, (i - 1) % tiles) for i in range(tiles)]
    halo = lax.ppermute(maps, "tile", ring)

    band_first = jnp.transpose(band_coef, (1, 0, 2))
    field = shape((slots, length, 2 * length), f32)
    table, coef, near_probe, near, own, far_edge, total_edge = pl.pallas_call(
        first_kernel,
        out_shape=(
            shape((slots, 3, length, length), bf16),
            shape((slots, 6 * materials, length), f32),
            shape(probe.shape, f32),
            shape(probe.shape, f32),
            shape(maps.shape, f32),
            field,
            square,
        ),
        in_specs=[ANY] * 6,
        out_specs=(VM,) * 7,
        scratch_shapes=[
            pltpu.SMEM(spectrum.shape, f32),
            pltpu.SMEM(wave_index.shape, jnp.int32),
            pltpu.SMEM(edge_band.shape[::-1], jnp.int32),
            pltpu.SMEM(band_first.shape, f32),
            pltpu.VMEM(maps.shape, f32),
            pltpu.VMEM((materials, half, length), f32),
            pltpu.SemaphoreType.DMA((6,)),
        ],
        compiler_params=params(),
        cost_estimate=pl.CostEstimate(flops=10**9, bytes_accessed=2**22, transcendentals=0),
        name="tables",
    )(*map(in_hbm, (spectrum, wave_index, edge_band.T, band_first, maps, probe)))
    edges = [total_edge]
    last = (tiles - 1) * count
    for k in range(1, count):
        pairs = [(last + w, last + (w ^ k)) for w in range(count)]
        edges.append(lax.ppermute(total_edge, ("tile", "wave"), pairs))
    here, power, left, right_root = pl.pallas_call(
        lambda *refs: power_kernel(count, *refs),
        out_shape=(share, square, square, square),
        in_specs=[ANY] * 2 + [VM] * 3,
        out_specs=(VM,) * 4,
        scratch_shapes=[
            pltpu.SMEM(offsets.shape, jnp.int32),
            pltpu.VMEM(measured.shape, f32),
            pltpu.SemaphoreType.DMA((2,)),
        ],
        compiler_params=params(),
        name="power",
    )(*map(in_hbm, (offsets, measured)), coef, near_probe, own)
    left_root = lax.ppermute(left, "tile", ring)
    message = shape((length + half_rows, length), f32)
    psi, far, *messages = pl.pallas_call(
        lambda *refs: forward_kernel(count, *refs),
        out_shape=(shape(probe.shape, f32), field) + (message,) * count,
        in_specs=[VM] * 6,
        out_specs=(VM,) * (2 + count),
        scratch_shapes=[
            pltpu.VMEM((materials, half, length), f32),
            pltpu.VMEM((length, length), f32),
        ],
        compiler_params=params(),
        name="forward",
    )(near, halo, near_probe, table, coef, power)
    shares = [messages[0]]
    for k in range(1, count):
        shares.append(lax.ppermute(messages[k], "wave", [(w, w ^ k) for w in range(count)]))

    *sends, scale = pl.pallas_call(
        lambda *refs: backward_kernel(tiles, count, *refs),
        out_shape=(share,) * count + (shape((half_rows, length), f32),),
        in_specs=[VM] * (7 + 2 * count),
        out_specs=(VM,) * (count + 1),
        scratch_shapes=[
            pltpu.VMEM((2 * length, length), f32),
            pltpu.VMEM((materials, length, length), f32),
            pltpu.VMEM((length, 2 * length), f32),
        ],
        compiler_params=params(),
        name="backward",
    )(right_root, left_root, table, coef, psi, far, far_edge, *shares, *edges)

    def owner(t, q):
        return (t + (q >= count // 2)) % tiles * count + q

    arrived = []
    for k in range(count):
        pairs = [(t * count + w, owner(t, w ^ k)) for t in range(tiles) for w in range(count)]
        arrived.append(lax.ppermute(sends[k], ("tile", "wave"), [p for p in pairs if p[0] != p[1]]))

    new = pl.pallas_call(
        lambda *refs: update_kernel(count, *refs),
        out_shape=share,
        in_specs=[VM] * (3 + count),
        out_specs=VM,
        compiler_params=params(),
        name="update",
    )(here, scale, sends[0], *arrived)

    parts = [new]
    for k in range(1, count):
        parts.append(lax.ppermute(new, "wave", [(w, w ^ k) for w in range(count)]))
    return pl.pallas_call(
        lambda *refs: join_kernel(count, *refs),
        out_shape=shape((materials, length, length), f32),
        in_specs=[VM] * count,
        out_specs=VM,
        compiler_params=params(),
        name="join",
    )(*parts)


def solution(mesh):
    in_specs = (
        P(None, None, "tile"),
        P("tile", None, None),
        P("tile"),
        P("wave", None, None, None),
        P("wave"),
        P("wave"),
        P("wave", None),
        P(),
    )
    out_specs = P(None, None, "tile")
    tiles, count = mesh.shape["tile"], mesh.shape["wave"]
    return jax.shard_map(
        lambda *args: per_device(tiles, count, *args),
        mesh=mesh,
        in_specs=in_specs,
        out_specs=out_specs,
        check_vma=False,
    )
```

```python
import math

import jax
import jax.numpy as jnp
import numpy as np
from jax import lax
from jax.experimental import pallas as pl
from jax.experimental.pallas import tpu as pltpu
from jax.sharding import PartitionSpec as P

WAVES = 48

relax = 4.0
floor_level = 1.0

UNROLL = 12
EDGE_UNROLL = 12
CHUNK = 32

VM = pl.BlockSpec(memory_space=pltpu.VMEM)
ANY = pl.BlockSpec(memory_space=pltpu.HBM)
f32 = jnp.float32
bf16 = jnp.bfloat16


def fit(parity, degree):
    nodes = 0.5 * np.cos(np.pi * (np.arange(400) + 0.5) / 800)
    turns = 2 * np.pi * nodes
    value = np.sin(turns) if parity else np.cos(turns)
    powers = np.stack([nodes ** (parity + 2 * i) for i in range(degree)], axis=1)
    return [float(c) for c in np.linalg.lstsq(powers, value, rcond=None)[0]]


SIN = fit(1, 6)
COS = fit(0, 7)


def horner(square, coefs):
    total = coefs[-1]
    for c in coefs[-2::-1]:
        total = total * square + c
    return total


def cos_sin(turns):
    r = turns - jnp.round(turns)
    square = r * r
    return horner(square, COS), horner(square, SIN) * r


def lanes(rows, length):
    return lax.broadcasted_iota(jnp.int32, (rows, length), 1)


def halves_packed(top, bottom, upper):
    length = top.shape[-1]
    half = length // 2
    low = lanes(top.shape[0], length) < half
    if upper:
        return jnp.where(low, pltpu.roll(top, half, 1), bottom)
    return jnp.where(low, top, pltpu.roll(bottom, half, 1))


def block(table_ref, s, kind):
    re, im, neg = table_ref[s, 0], table_ref[s, 1], table_ref[s, 2]
    top, bottom = ((re, neg), (im, re)) if kind == "L" else ((re, im), (neg, re))
    return jnp.concatenate(
        [jnp.concatenate(top, axis=1), jnp.concatenate(bottom, axis=1)], axis=0
    )


def piece(array, q, count, half_rows):
    groups = count // 2
    rows = 2 * half_rows
    start = pl.multiple_of(lax.rem(q, groups) * rows, half_rows)
    top = array[pl.ds(start, half_rows), :]
    bottom = array[pl.ds(start + half_rows, half_rows), :]
    return jnp.where(
        q < groups, halves_packed(top, bottom, False), halves_packed(top, bottom, True)
    )


def first_kernel(
    spectrum_any, wave_any, edge_any, band_any, maps_any, probe_any,
    table, coef, probe, near, own, far_edge, total_edge,
    spectrum, wave_index, edge_band, band_coef, maps, packed, sems,
):
    copies = [
        pltpu.make_async_copy(source, target, sems.at[i])
        for i, (source, target) in enumerate(
            (
                (wave_any, wave_index),
                (edge_any, edge_band),
                (band_any, band_coef),
                (spectrum_any, spectrum),
                (maps_any, maps),
                (probe_any, probe),
            )
        )
    ]
    for copy in copies:
        copy.start()
    materials, length, _ = maps.shape
    half = length // 2
    slots = probe.shape[0]
    group = 8
    centred_lane = (lanes(group, length) - half).astype(f32)
    row = lax.broadcasted_iota(jnp.int32, (group, length), 0)
    fine = row.astype(f32) * centred_lane / length
    normaliser = 1.0 / math.sqrt(length)
    coarse_rows = length // group
    copies[0].wait()

    def tables(s, carry):
        which = jnp.full((group, length), wave_index[s], jnp.int32).astype(f32)
        sampling = 0.6 + 0.4 * which / (WAVES - 1)
        fine_cos, fine_sin = cos_sin(sampling * fine)
        fine_cos, fine_sin = fine_cos * normaliser, fine_sin * normaliser
        for base in range(0, coarse_rows, group):
            step = ((row + base) * group - half).astype(f32) * centred_lane / length
            cos, sin = cos_sin(sampling * step)
            for i in range(0, group, 2):
                parts = []
                for j in (i, i + 1):
                    c = jnp.broadcast_to(cos[j : j + 1], (group, length))
                    n = jnp.broadcast_to(sin[j : j + 1], (group, length))
                    parts.append((c * fine_cos - n * fine_sin, n * fine_cos + c * fine_sin))
                at = pl.ds((base + i) * group, 2 * group)
                re = jnp.concatenate([parts[0][0], parts[1][0]], axis=0).astype(bf16)
                positive = jnp.concatenate([parts[0][1], parts[1][1]], axis=0)
                table[s, 0, at, :] = re
                table[s, 1, at, :] = (-positive).astype(bf16)
                table[s, 2, at, :] = positive.astype(bf16)
        return carry

    lax.fori_loop(0, slots, tables, 0, unroll=2)

    for copy in copies[1:]:
        copy.wait()
    for s in range(slots):
        for m in range(materials):
            band = edge_band[m, s]
            a, b = band_coef[band, 0, m], band_coef[band, 1, m]
            coef[s, m, :] = jnp.full((length,), a * (-math.log2(math.e)), f32)
            coef[s, materials + m, :] = jnp.full((length,), b * (0.5 / math.pi), f32)
            coef[s, 2 * materials + m, :] = jnp.full((length,), a, f32)
            coef[s, 3 * materials + m, :] = jnp.full((length,), b, f32)
        coef[s, 4 * materials, :] = jnp.full((length,), spectrum[s], f32)
    for m in range(materials):
        own[m] = pltpu.roll(maps[m], half, 1)
        packed[m] = halves_packed(own[m, :half], own[m, half:], False)

    def near_object(s, carry):
        for start in range(0, half, CHUNK):
            parts = object_of(coef, s, [packed[m, start : start + CHUNK] for m in range(materials)])
            for i, part in enumerate(parts):
                near[s, i, start : start + CHUNK] = part
                near[s, i, half + start : half + start + CHUNK] = pltpu.roll(part, half, 1)
        return carry

    lax.fori_loop(0, slots, near_object, 0, unroll=2)

    @pl.when(lax.axis_index("tile") == lax.axis_size("tile") - 1)
    def _():
        total_edge[...] = jnp.zeros_like(total_edge)
        low = lanes(length, length) < half

        def step(s, carry):
            re, im, cos, sin = probe[s, 0], probe[s, 1], near[s, 0], near[s, 1]
            field = [
                (jnp.where(low, re * cos - im * sin, re), jnp.where(low, re * sin + im * cos, im))
            ]
            got = transform(block(table, s, "L"), block(table, s, "R"), field)
            far_edge[s] = got
            re, im = got[:, :length], got[:, length:]
            total_edge[...] += coef[s, 4 * materials : 4 * materials + 1] * (re * re + im * im)
            return carry

        lax.fori_loop(0, slots, step, 0, unroll=EDGE_UNROLL)


def power_kernel(
    count, offsets_any, measured_any, coef, probe, own,
    here, power, left_root, right_root,
    offsets, measured, sems,
):
    copies = [
        pltpu.make_async_copy(source, target, sems.at[i])
        for i, (source, target) in enumerate(((offsets_any, offsets), (measured_any, measured)))
    ]
    for copy in copies:
        copy.start()
    materials, length, _ = own.shape
    half = length // 2
    slots = probe.shape[0]
    tile, tiles = lax.axis_index("tile"), lax.axis_size("tile")
    me = lax.axis_index("wave")
    low = lanes(CHUNK, length) < half
    frames = jnp.where(
        low,
        jnp.where(tile == tiles - 1, 1.0, 2.0),
        jnp.where(tile == 0, 1.0, 2.0),
    )
    for start in range(0, length, CHUNK):
        at = slice(start, start + CHUNK)
        window = [own[m, at] for m in range(materials)]

        def add(s, total):
            absorb = None
            for m in range(materials):
                term = coef[s, m : m + 1] * window[m]
                absorb = term if absorb is None else absorb + term
            re, im = probe[s, 0, at], probe[s, 1, at]
            weight = coef[s, 4 * materials : 4 * materials + 1]
            return total + (weight * jnp.exp2(absorb + absorb)) * (re * re + im * im)

        total = lax.fori_loop(0, slots, add, jnp.zeros((CHUNK, length), f32), unroll=4)
        power[at] = frames * total
    half_rows = length // count
    for m in range(materials):
        here[m] = piece(own.at[m], me, count, half_rows)
    for copy in copies:
        copy.wait()
    left_first = offsets[0] < offsets[1]
    first, second = jnp.sqrt(measured[0]), jnp.sqrt(measured[1])
    left_root[...] = jnp.where(left_first, first, second)
    right_root[...] = jnp.where(left_first, second, first)


def object_of(coef, s, window):
    materials = len(window)
    absorb, phase = None, None
    for m, w in enumerate(window):
        a = coef[s, m : m + 1] * w
        b = coef[s, materials + m : materials + m + 1] * w
        absorb = a if absorb is None else absorb + a
        phase = b if phase is None else phase + b
    damping = jnp.exp2(absorb)
    cos, sin = cos_sin(phase)
    return damping * cos, damping * sin


def transform(left, right, fields):
    length = fields[0][0].shape[0]
    stacked = jnp.concatenate(
        [jnp.concatenate([re.astype(bf16), im.astype(bf16)], axis=0) for re, im in fields], axis=1
    )
    mid = jnp.dot(left, stacked, preferred_element_type=f32).astype(bf16)
    beside = jnp.concatenate(
        [
            jnp.concatenate(
                [mid[:length, i * length : (i + 1) * length], mid[length:, i * length : (i + 1) * length]], axis=1
            )
            for i in range(len(fields))
        ],
        axis=0,
    )
    if len(fields) == 1:
        beside = jnp.concatenate([beside, beside], axis=0)
    return jnp.dot(beside, right, preferred_element_type=f32)[: len(fields) * length]


def forward_kernel(count, near, halo, probe, table, coef, power, psi, far, *rest):
    messages, (beyond, total) = rest[:count], rest[count:]
    materials, length, _ = halo.shape
    half = length // 2
    slots = probe.shape[0]
    me = lax.axis_index("wave")
    for m in range(materials):
        beyond[m] = halves_packed(halo[m, :half], halo[m, half:], False)
    total[...] = jnp.zeros_like(total)
    low = lanes(CHUNK, length) < half

    def exit_wave(s):
        for start in range(0, half, CHUNK):
            parts = object_of(coef, s, [beyond[m, start : start + CHUNK] for m in range(materials)])
            upper, lower = slice(start, start + CHUNK), slice(half + start, half + start + CHUNK)
            for at, turned in ((upper, True), (lower, False)):
                cos, sin = [
                    jnp.where(low, near[s, i, at], pltpu.roll(part, half, 1) if turned else part)
                    for i, part in enumerate(parts)
                ]
                re, im = probe[s, 0, at], probe[s, 1, at]
                psi[s, 0, at] = re * cos - im * sin
                psi[s, 1, at] = re * sin + im * cos

    def step(s, joined):
        exit_wave(s)
        re, im = psi[s, 0], psi[s, 1]
        if joined:
            low = lanes(length, length) < half
            re, im = jnp.where(low, probe[s, 0], re), jnp.where(low, probe[s, 1], im)
        got = transform(block(table, s, "L"), block(table, s, "R"), [(re, im)])
        far[s] = got
        re, im = got[:, :length], got[:, length:]
        total[...] += coef[s, 4 * materials : 4 * materials + 1] * (re * re + im * im)

    edge = lax.axis_index("tile") == lax.axis_size("tile") - 1
    for joined in (False, True):

        @pl.when(edge == joined)
        def _():
            lax.fori_loop(
                0, slots, lambda s, c: (step(s, joined), c)[1], 0, unroll=EDGE_UNROLL if joined else UNROLL
            )

    half_rows = length // count
    for k, message in enumerate(messages):
        message[:length] = total[...]
        message[length:] = piece(power, jnp.bitwise_xor(me, k), count, half_rows)


def backward_kernel(tiles, count, right_root, left_root, table, coef, psi, far, far_edge, *rest):
    shares, rest = rest[:count], rest[count:]
    edges, rest = rest[:count], rest[count:]
    sends, rest = rest[:count], rest[count:]
    scale, shortfall, gradient, back = rest
    length = right_root.shape[0]
    materials = gradient.shape[0]
    half = length // 2
    slots = psi.shape[0]
    edge = lax.axis_index("tile") == tiles - 1
    me = lax.axis_index("wave")
    half_rows = length // count
    powers = shares[0][length:]
    for share in shares[1:]:
        powers = powers + share[length:]
    scale[...] = relax / (powers + 1.0)
    gradient[...] = jnp.zeros_like(gradient)

    def inverse(shares):
        intensity = shares[0][:length]
        for share in shares[1:]:
            intensity = intensity + share[:length]
        return lax.rsqrt(jnp.maximum(intensity, floor_level))

    def delta(s, far, at):
        factor = coef[s, 4 * materials : 4 * materials + 1] * shortfall[at : at + length]
        return factor * far[s, :, :length], factor * far[s, :, length:]

    def collect(s):
        for start in range(0, length, CHUNK):
            at = slice(start, start + CHUNK)
            re, im = psi[s, 0, at], psi[s, 1, at]
            back_re, back_im = back[at, :length], back[at, length:]
            cross_re = re * back_re + im * back_im
            cross_im = re * back_im - im * back_re
            for m in range(materials):
                a = coef[s, 2 * materials + m : 2 * materials + m + 1]
                b = coef[s, 3 * materials + m : 3 * materials + m + 1]
                gradient[m, at] += b * cross_im - a * cross_re

    @pl.when(jnp.logical_not(edge))
    def _():
        shortfall[:length] = (right_root[...] + left_root[...]) * inverse(shares) - 2.0

        def step(s, carry):
            back[...] = transform(block(table, s, "R"), block(table, s, "L"), [delta(s, far, 0)])
            collect(s)
            return carry

        lax.fori_loop(0, slots, step, 0, unroll=UNROLL)

    @pl.when(edge)
    def _():
        shortfall[:length] = left_root[...] * inverse(shares) - 1.0
        shortfall[length:] = right_root[...] * inverse(edges) - 1.0
        low = (lax.broadcasted_iota(jnp.int32, (length, 2 * length), 1) & (length - 1)) < half

        def step(s, carry):
            both = transform(
                block(table, s, "R"), block(table, s, "L"), [delta(s, far, 0), delta(s, far_edge, length)]
            )
            back[...] = jnp.where(low, both[length:], both[:length])
            collect(s)
            return carry

        lax.fori_loop(0, slots, step, 0, unroll=EDGE_UNROLL)

    for k, send in enumerate(sends):
        for m in range(materials):
            send[m] = piece(gradient.at[m], jnp.bitwise_xor(me, k), count, half_rows)


def update_kernel(count, here, scale, *refs):
    own, arrived, out = refs[0], refs[1:-1], refs[-1]
    me = lax.axis_index("wave")
    for m in range(here.shape[0]):
        total = jnp.where(me < count // 2, own[m], arrived[0][m])
        for other in arrived[1:]:
            total = total + other[m]
        out[m] = here[m] + scale[...] * total


def join_kernel(count, *refs):
    shares, out = refs[:count], refs[count]
    materials, length, _ = out.shape
    half = length // 2
    me = lax.axis_index("wave")
    half_rows = length // count
    groups = count // 2
    low = lanes(half_rows, length) < half
    for position in range(count):

        @pl.when(me == position)
        def _():
            held = lambda q: shares[q ^ position]
            for g in range(groups):
                right, left = held(g), held(g + groups)
                start = g * 2 * half_rows
                for m in range(materials):
                    r, l = right[m], left[m]
                    out[m, start : start + half_rows] = jnp.where(low, l, pltpu.roll(r, half, 1))
                    out[m, start + half_rows : start + 2 * half_rows] = jnp.where(
                        low, pltpu.roll(l, half, 1), r
                    )


def in_hbm(array):
    return pltpu.with_memory_space_constraint(array, pltpu.HBM)


def params(mib=40):
    return pltpu.CompilerParams(vmem_limit_bytes=mib * 2**20)


def per_device(tiles, count, maps, measured, offsets, probe, spectrum, wave_index, edge_band, band_coef):
    materials, length, columns = maps.shape
    slots = probe.shape[0]
    half = length // 2
    shape = jax.ShapeDtypeStruct
    half_rows = length // count
    square = shape((length, length), f32)
    share = shape((materials, half_rows, length), f32)

    ring = [(i, (i - 1) % tiles) for i in range(tiles)]
    halo = lax.ppermute(maps, "tile", ring)

    band_first = jnp.transpose(band_coef, (1, 0, 2))
    field = shape((slots, length, 2 * length), f32)
    table, coef, near_probe, near, own, far_edge, total_edge = pl.pallas_call(
        first_kernel,
        out_shape=(
            shape((slots, 3, length, length), bf16),
            shape((slots, 6 * materials, length), f32),
            shape(probe.shape, f32),
            shape(probe.shape, f32),
            shape(maps.shape, f32),
            field,
            square,
        ),
        in_specs=[ANY] * 6,
        out_specs=(VM,) * 7,
        scratch_shapes=[
            pltpu.SMEM(spectrum.shape, f32),
            pltpu.SMEM(wave_index.shape, jnp.int32),
            pltpu.SMEM(edge_band.shape[::-1], jnp.int32),
            pltpu.SMEM(band_first.shape, f32),
            pltpu.VMEM(maps.shape, f32),
            pltpu.VMEM((materials, half, length), f32),
            pltpu.SemaphoreType.DMA((6,)),
        ],
        compiler_params=params(),
        cost_estimate=pl.CostEstimate(flops=10**9, bytes_accessed=2**22, transcendentals=0),
        name="tables",
    )(*map(in_hbm, (spectrum, wave_index, edge_band.T, band_first, maps, probe)))
    edges = [total_edge]
    last = (tiles - 1) * count
    for k in range(1, count):
        pairs = [(last + w, last + (w ^ k)) for w in range(count)]
        edges.append(lax.ppermute(total_edge, ("tile", "wave"), pairs))
    here, power, left, right_root = pl.pallas_call(
        lambda *refs: power_kernel(count, *refs),
        out_shape=(share, square, square, square),
        in_specs=[ANY] * 2 + [VM] * 3,
        out_specs=(VM,) * 4,
        scratch_shapes=[
            pltpu.SMEM(offsets.shape, jnp.int32),
            pltpu.VMEM(measured.shape, f32),
            pltpu.SemaphoreType.DMA((2,)),
        ],
        compiler_params=params(),
        name="power",
    )(*map(in_hbm, (offsets, measured)), coef, near_probe, own)
    left_root = lax.ppermute(left, "tile", ring)
    message = shape((length + half_rows, length), f32)
    psi, far, *messages = pl.pallas_call(
        lambda *refs: forward_kernel(count, *refs),
        out_shape=(shape(probe.shape, f32), field) + (message,) * count,
        in_specs=[VM] * 6,
        out_specs=(VM,) * (2 + count),
        scratch_shapes=[
            pltpu.VMEM((materials, half, length), f32),
            pltpu.VMEM((length, length), f32),
        ],
        compiler_params=params(),
        name="forward",
    )(near, halo, near_probe, table, coef, power)
    shares = [messages[0]]
    for k in range(1, count):
        shares.append(lax.ppermute(messages[k], "wave", [(w, w ^ k) for w in range(count)]))

    *sends, scale = pl.pallas_call(
        lambda *refs: backward_kernel(tiles, count, *refs),
        out_shape=(share,) * count + (shape((half_rows, length), f32),),
        in_specs=[VM] * (7 + 2 * count),
        out_specs=(VM,) * (count + 1),
        scratch_shapes=[
            pltpu.VMEM((2 * length, length), f32),
            pltpu.VMEM((materials, length, length), f32),
            pltpu.VMEM((length, 2 * length), f32),
        ],
        compiler_params=params(),
        name="backward",
    )(right_root, left_root, table, coef, psi, far, far_edge, *shares, *edges)

    def owner(t, q):
        return (t + (q >= count // 2)) % tiles * count + q

    arrived = []
    for k in range(count):
        pairs = [(t * count + w, owner(t, w ^ k)) for t in range(tiles) for w in range(count)]
        arrived.append(lax.ppermute(sends[k], ("tile", "wave"), [p for p in pairs if p[0] != p[1]]))

    new = pl.pallas_call(
        lambda *refs: update_kernel(count, *refs),
        out_shape=share,
        in_specs=[VM] * (3 + count),
        out_specs=VM,
        compiler_params=params(),
        name="update",
    )(here, scale, sends[0], *arrived)

    parts = [new]
    for k in range(1, count):
        parts.append(lax.ppermute(new, "wave", [(w, w ^ k) for w in range(count)]))
    return pl.pallas_call(
        lambda *refs: join_kernel(count, *refs),
        out_shape=shape((materials, length, length), f32),
        in_specs=[VM] * count,
        out_specs=VM,
        compiler_params=params(),
        name="join",
    )(*parts)


def solution(mesh):
    in_specs = (
        P(None, None, "tile"),
        P("tile", None, None),
        P("tile"),
        P("wave", None, None, None),
        P("wave"),
        P("wave"),
        P("wave", None),
        P(),
    )
    out_specs = P(None, None, "tile")
    tiles, count = mesh.shape["tile"], mesh.shape["wave"]
    return jax.shard_map(
        lambda *args: per_device(tiles, count, *args),
        mesh=mesh,
        in_specs=in_specs,
        out_specs=out_specs,
        check_vma=False,
    )
```

```python
import math

import jax
import jax.numpy as jnp
import numpy as np
from jax import lax
from jax.experimental import pallas as pl
from jax.experimental.pallas import tpu as pltpu
from jax.sharding import PartitionSpec as P

WAVES = 48

relax = 4.0
floor_level = 1.0

UNROLL = 12
EDGE_UNROLL = 12
CHUNK = 32

VM = pl.BlockSpec(memory_space=pltpu.VMEM)
ANY = pl.BlockSpec(memory_space=pltpu.HBM)
f32 = jnp.float32
bf16 = jnp.bfloat16


def fit(parity, degree):
    nodes = 0.5 * np.cos(np.pi * (np.arange(400) + 0.5) / 800)
    turns = 2 * np.pi * nodes
    value = np.sin(turns) if parity else np.cos(turns)
    powers = np.stack([nodes ** (parity + 2 * i) for i in range(degree)], axis=1)
    return [float(c) for c in np.linalg.lstsq(powers, value, rcond=None)[0]]


SIN = fit(1, 6)
COS = fit(0, 7)


def horner(square, coefs):
    total = coefs[-1]
    for c in coefs[-2::-1]:
        total = total * square + c
    return total


def cos_sin(turns):
    r = turns - jnp.round(turns)
    square = r * r
    return horner(square, COS), horner(square, SIN) * r


def lanes(rows, length):
    return lax.broadcasted_iota(jnp.int32, (rows, length), 1)


def halves_packed(top, bottom, upper):
    length = top.shape[-1]
    half = length // 2
    low = lanes(top.shape[0], length) < half
    if upper:
        return jnp.where(low, pltpu.roll(top, half, 1), bottom)
    return jnp.where(low, top, pltpu.roll(bottom, half, 1))


def block(table_ref, s, kind):
    re, im, neg = table_ref[s, 0], table_ref[s, 1], table_ref[s, 2]
    top, bottom = ((re, neg), (im, re)) if kind == "L" else ((re, im), (neg, re))
    return jnp.concatenate(
        [jnp.concatenate(top, axis=1), jnp.concatenate(bottom, axis=1)], axis=0
    )


def piece(array, q, count, half_rows):
    groups = count // 2
    rows = 2 * half_rows
    start = pl.multiple_of(lax.rem(q, groups) * rows, half_rows)
    top = array[pl.ds(start, half_rows), :]
    bottom = array[pl.ds(start + half_rows, half_rows), :]
    return jnp.where(
        q < groups, halves_packed(top, bottom, False), halves_packed(top, bottom, True)
    )


def first_kernel(
    spectrum_any, wave_any, edge_any, band_any, maps_any, probe_any,
    table, coef, probe, near, own, far_edge, total_edge,
    spectrum, wave_index, edge_band, band_coef, maps, packed, sems,
):
    copies = [
        pltpu.make_async_copy(source, target, sems.at[i])
        for i, (source, target) in enumerate(
            (
                (wave_any, wave_index),
                (edge_any, edge_band),
                (band_any, band_coef),
                (spectrum_any, spectrum),
                (maps_any, maps),
                (probe_any, probe),
            )
        )
    ]
    for copy in copies:
        copy.start()
    materials, length, _ = maps.shape
    half = length // 2
    slots = probe.shape[0]
    group = 8
    centred_lane = (lanes(group, length) - half).astype(f32)
    row = lax.broadcasted_iota(jnp.int32, (group, length), 0)
    fine = row.astype(f32) * centred_lane / length
    normaliser = 1.0 / math.sqrt(length)
    coarse_rows = length // group
    copies[0].wait()

    def tables(s, carry):
        which = jnp.full((group, length), wave_index[s], jnp.int32).astype(f32)
        sampling = 0.6 + 0.4 * which / (WAVES - 1)
        fine_cos, fine_sin = cos_sin(sampling * fine)
        fine_cos, fine_sin = fine_cos * normaliser, fine_sin * normaliser
        for base in range(0, coarse_rows, group):
            step = ((row + base) * group - half).astype(f32) * centred_lane / length
            cos, sin = cos_sin(sampling * step)
            for i in range(0, group, 2):
                parts = []
                for j in (i, i + 1):
                    c = jnp.broadcast_to(cos[j : j + 1], (group, length))
                    n = jnp.broadcast_to(sin[j : j + 1], (group, length))
                    parts.append((c * fine_cos - n * fine_sin, n * fine_cos + c * fine_sin))
                at = pl.ds((base + i) * group, 2 * group)
                re = jnp.concatenate([parts[0][0], parts[1][0]], axis=0).astype(bf16)
                positive = jnp.concatenate([parts[0][1], parts[1][1]], axis=0)
                table[s, 0, at, :] = re
                table[s, 1, at, :] = (-positive).astype(bf16)
                table[s, 2, at, :] = positive.astype(bf16)
        return carry

    lax.fori_loop(0, slots, tables, 0, unroll=2)

    for copy in copies[1:]:
        copy.wait()
    for s in range(slots):
        for m in range(materials):
            band = edge_band[m, s]
            a, b = band_coef[band, 0, m], band_coef[band, 1, m]
            coef[s, m, :] = jnp.full((length,), a * (-math.log2(math.e)), f32)
            coef[s, materials + m, :] = jnp.full((length,), b * (0.5 / math.pi), f32)
            coef[s, 2 * materials + m, :] = jnp.full((length,), a, f32)
            coef[s, 3 * materials + m, :] = jnp.full((length,), b, f32)
        coef[s, 4 * materials, :] = jnp.full((length,), spectrum[s], f32)
    for m in range(materials):
        own[m] = pltpu.roll(maps[m], half, 1)
        packed[m] = halves_packed(own[m, :half], own[m, half:], False)

    def near_object(s, carry):
        for start in range(0, half, CHUNK):
            parts = object_of(coef, s, [packed[m, start : start + CHUNK] for m in range(materials)])
            for i, part in enumerate(parts):
                near[s, i, start : start + CHUNK] = part
                near[s, i, half + start : half + start + CHUNK] = pltpu.roll(part, half, 1)
        return carry

    lax.fori_loop(0, slots, near_object, 0, unroll=2)

    @pl.when(lax.axis_index("tile") == lax.axis_size("tile") - 1)
    def _():
        total_edge[...] = jnp.zeros_like(total_edge)
        low = lanes(length, length) < half

        def step(s, carry):
            re, im, cos, sin = probe[s, 0], probe[s, 1], near[s, 0], near[s, 1]
            field = [
                (jnp.where(low, re * cos - im * sin, re), jnp.where(low, re * sin + im * cos, im))
            ]
            got = transform(block(table, s, "L"), block(table, s, "R"), field)
            far_edge[s] = got
            re, im = got[:, :length], got[:, length:]
            total_edge[...] += coef[s, 4 * materials : 4 * materials + 1] * (re * re + im * im)
            return carry

        lax.fori_loop(0, slots, step, 0, unroll=EDGE_UNROLL)


def power_kernel(
    count, offsets_any, measured_any, coef, probe, own,
    here, power, left_root, right_root,
    offsets, measured, sems,
):
    copies = [
        pltpu.make_async_copy(source, target, sems.at[i])
        for i, (source, target) in enumerate(((offsets_any, offsets), (measured_any, measured)))
    ]
    for copy in copies:
        copy.start()
    materials, length, _ = own.shape
    half = length // 2
    slots = probe.shape[0]
    tile, tiles = lax.axis_index("tile"), lax.axis_size("tile")
    me = lax.axis_index("wave")
    low = lanes(CHUNK, length) < half
    frames = jnp.where(
        low,
        jnp.where(tile == tiles - 1, 1.0, 2.0),
        jnp.where(tile == 0, 1.0, 2.0),
    )
    for start in range(0, length, CHUNK):
        at = slice(start, start + CHUNK)
        window = [own[m, at] for m in range(materials)]

        def add(s, total):
            absorb = None
            for m in range(materials):
                term = coef[s, m : m + 1] * window[m]
                absorb = term if absorb is None else absorb + term
            re, im = probe[s, 0, at], probe[s, 1, at]
            weight = coef[s, 4 * materials : 4 * materials + 1]
            return total + (weight * jnp.exp2(absorb + absorb)) * (re * re + im * im)

        total = lax.fori_loop(0, slots, add, jnp.zeros((CHUNK, length), f32), unroll=4)
        power[at] = frames * total
    half_rows = length // count
    for m in range(materials):
        here[m] = piece(own.at[m], me, count, half_rows)
    for copy in copies:
        copy.wait()
    left_first = offsets[0] < offsets[1]
    first, second = jnp.sqrt(measured[0]), jnp.sqrt(measured[1])
    left_root[...] = jnp.where(left_first, first, second)
    right_root[...] = jnp.where(left_first, second, first)


def object_of(coef, s, window):
    materials = len(window)
    absorb, phase = None, None
    for m, w in enumerate(window):
        a = coef[s, m : m + 1] * w
        b = coef[s, materials + m : materials + m + 1] * w
        absorb = a if absorb is None else absorb + a
        phase = b if phase is None else phase + b
    damping = jnp.exp2(absorb)
    cos, sin = cos_sin(phase)
    return damping * cos, damping * sin


def transform(left, right, fields):
    length = fields[0][0].shape[0]
    stacked = jnp.concatenate(
        [jnp.concatenate([re.astype(bf16), im.astype(bf16)], axis=0) for re, im in fields], axis=1
    )
    mid = jnp.dot(left, stacked, preferred_element_type=f32).astype(bf16)
    beside = jnp.concatenate(
        [
            jnp.concatenate(
                [mid[:length, i * length : (i + 1) * length], mid[length:, i * length : (i + 1) * length]], axis=1
            )
            for i in range(len(fields))
        ],
        axis=0,
    )
    if len(fields) == 1:
        beside = jnp.concatenate([beside, beside], axis=0)
    return jnp.dot(beside, right, preferred_element_type=f32)[: len(fields) * length]


def forward_kernel(
    count, near, halo, probe, table, coef, power, total_edge, other_edge, psi, far, pair_edge, *rest
):
    messages, (beyond, total) = rest[:count], rest[count:]
    materials, length, _ = halo.shape
    half = length // 2
    slots = probe.shape[0]
    me = lax.axis_index("wave")
    for m in range(materials):
        beyond[m] = halves_packed(halo[m, :half], halo[m, half:], False)
    total[...] = jnp.zeros_like(total)
    low = lanes(CHUNK, length) < half

    def exit_wave(s):
        for start in range(0, half, CHUNK):
            parts = object_of(coef, s, [beyond[m, start : start + CHUNK] for m in range(materials)])
            upper, lower = slice(start, start + CHUNK), slice(half + start, half + start + CHUNK)
            for at, turned in ((upper, True), (lower, False)):
                cos, sin = [
                    jnp.where(low, near[s, i, at], pltpu.roll(part, half, 1) if turned else part)
                    for i, part in enumerate(parts)
                ]
                re, im = probe[s, 0, at], probe[s, 1, at]
                psi[s, 0, at] = re * cos - im * sin
                psi[s, 1, at] = re * sin + im * cos

    def step(s, joined):
        exit_wave(s)
        re, im = psi[s, 0], psi[s, 1]
        if joined:
            low = lanes(length, length) < half
            re, im = jnp.where(low, probe[s, 0], re), jnp.where(low, probe[s, 1], im)
        got = transform(block(table, s, "L"), block(table, s, "R"), [(re, im)])
        far[s] = got
        re, im = got[:, :length], got[:, length:]
        total[...] += coef[s, 4 * materials : 4 * materials + 1] * (re * re + im * im)

    edge = lax.axis_index("tile") == lax.axis_size("tile") - 1

    @pl.when(edge)
    def _():
        pair_edge[...] = total_edge[...] + other_edge[...]

    for joined in (False, True):

        @pl.when(edge == joined)
        def _():
            lax.fori_loop(
                0, slots, lambda s, c: (step(s, joined), c)[1], 0, unroll=EDGE_UNROLL if joined else UNROLL
            )

    half_rows = length // count
    for k, message in enumerate(messages):
        message[:length] = total[...]
        message[length:] = piece(power, jnp.bitwise_xor(me, k), count, half_rows)


def backward_kernel(tiles, count, right_root, left_root, table, coef, psi, far, far_edge, *rest):
    shares, rest = rest[:count], rest[count:]
    edges, rest = rest[: count // 2], rest[count // 2 :]
    sends, rest = rest[:count], rest[count:]
    scale, shortfall, gradient, back = rest
    length = right_root.shape[0]
    materials = gradient.shape[0]
    half = length // 2
    slots = psi.shape[0]
    edge = lax.axis_index("tile") == tiles - 1
    me = lax.axis_index("wave")
    half_rows = length // count
    powers = shares[0][length:]
    for share in shares[1:]:
        powers = powers + share[length:]
    scale[...] = relax / (powers + 1.0)
    gradient[...] = jnp.zeros_like(gradient)

    def inverse(shares):
        intensity = shares[0][:length]
        for share in shares[1:]:
            intensity = intensity + share[:length]
        return lax.rsqrt(jnp.maximum(intensity, floor_level))

    def delta(s, far, at):
        factor = coef[s, 4 * materials : 4 * materials + 1] * shortfall[at : at + length]
        return factor * far[s, :, :length], factor * far[s, :, length:]

    def collect(s):
        for start in range(0, length, CHUNK):
            at = slice(start, start + CHUNK)
            re, im = psi[s, 0, at], psi[s, 1, at]
            back_re, back_im = back[at, :length], back[at, length:]
            cross_re = re * back_re + im * back_im
            cross_im = re * back_im - im * back_re
            for m in range(materials):
                a = coef[s, 2 * materials + m : 2 * materials + m + 1]
                b = coef[s, 3 * materials + m : 3 * materials + m + 1]
                gradient[m, at] += b * cross_im - a * cross_re

    @pl.when(jnp.logical_not(edge))
    def _():
        shortfall[:length] = (right_root[...] + left_root[...]) * inverse(shares) - 2.0

        def step(s, carry):
            back[...] = transform(block(table, s, "R"), block(table, s, "L"), [delta(s, far, 0)])
            collect(s)
            return carry

        lax.fori_loop(0, slots, step, 0, unroll=UNROLL)

    @pl.when(edge)
    def _():
        shortfall[:length] = left_root[...] * inverse(shares) - 1.0
        shortfall[length:] = right_root[...] * inverse(edges) - 1.0
        low = (lax.broadcasted_iota(jnp.int32, (length, 2 * length), 1) & (length - 1)) < half

        def step(s, carry):
            both = transform(
                block(table, s, "R"), block(table, s, "L"), [delta(s, far, 0), delta(s, far_edge, length)]
            )
            back[...] = jnp.where(low, both[length:], both[:length])
            collect(s)
            return carry

        lax.fori_loop(0, slots, step, 0, unroll=EDGE_UNROLL)

    for k, send in enumerate(sends):
        for m in range(materials):
            send[m] = piece(gradient.at[m], jnp.bitwise_xor(me, k), count, half_rows)


def update_kernel(count, here, scale, *refs):
    own, arrived, out = refs[0], refs[1:-1], refs[-1]
    me = lax.axis_index("wave")
    for m in range(here.shape[0]):
        total = jnp.where(me < count // 2, own[m], arrived[0][m])
        for other in arrived[1:]:
            total = total + other[m]
        out[m] = here[m] + scale[...] * total


def join_kernel(count, *refs):
    shares, out = refs[:count], refs[count]
    materials, length, _ = out.shape
    half = length // 2
    me = lax.axis_index("wave")
    half_rows = length // count
    groups = count // 2
    low = lanes(half_rows, length) < half
    for position in range(count):

        @pl.when(me == position)
        def _():
            held = lambda q: shares[q ^ position]
            for g in range(groups):
                right, left = held(g), held(g + groups)
                start = g * 2 * half_rows
                for m in range(materials):
                    r, l = right[m], left[m]
                    out[m, start : start + half_rows] = jnp.where(low, l, pltpu.roll(r, half, 1))
                    out[m, start + half_rows : start + 2 * half_rows] = jnp.where(
                        low, pltpu.roll(l, half, 1), r
                    )


def in_hbm(array):
    return pltpu.with_memory_space_constraint(array, pltpu.HBM)


def params(mib=40):
    return pltpu.CompilerParams(vmem_limit_bytes=mib * 2**20)


def per_device(tiles, count, maps, measured, offsets, probe, spectrum, wave_index, edge_band, band_coef):
    materials, length, columns = maps.shape
    slots = probe.shape[0]
    half = length // 2
    shape = jax.ShapeDtypeStruct
    half_rows = length // count
    square = shape((length, length), f32)
    share = shape((materials, half_rows, length), f32)

    ring = [(i, (i - 1) % tiles) for i in range(tiles)]
    halo = lax.ppermute(maps, "tile", ring)

    band_first = jnp.transpose(band_coef, (1, 0, 2))
    field = shape((slots, length, 2 * length), f32)
    table, coef, near_probe, near, own, far_edge, total_edge = pl.pallas_call(
        first_kernel,
        out_shape=(
            shape((slots, 3, length, length), bf16),
            shape((slots, 6 * materials, length), f32),
            shape(probe.shape, f32),
            shape(probe.shape, f32),
            shape(maps.shape, f32),
            field,
            square,
        ),
        in_specs=[ANY] * 6,
        out_specs=(VM,) * 7,
        scratch_shapes=[
            pltpu.SMEM(spectrum.shape, f32),
            pltpu.SMEM(wave_index.shape, jnp.int32),
            pltpu.SMEM(edge_band.shape[::-1], jnp.int32),
            pltpu.SMEM(band_first.shape, f32),
            pltpu.VMEM(maps.shape, f32),
            pltpu.VMEM((materials, half, length), f32),
            pltpu.SemaphoreType.DMA((6,)),
        ],
        compiler_params=params(),
        cost_estimate=pl.CostEstimate(flops=10**9, bytes_accessed=2**22, transcendentals=0),
        name="tables",
    )(*map(in_hbm, (spectrum, wave_index, edge_band.T, band_first, maps, probe)))
    both = ("tile", "wave")
    last = (tiles - 1) * count

    def among_last(array, k):
        return lax.ppermute(array, both, [(last + w, last + (w ^ k)) for w in range(count)])

    other_edge = among_last(total_edge, 1)
    here, power, left, right_root = pl.pallas_call(
        lambda *refs: power_kernel(count, *refs),
        out_shape=(share, square, square, square),
        in_specs=[ANY] * 2 + [VM] * 3,
        out_specs=(VM,) * 4,
        scratch_shapes=[
            pltpu.SMEM(offsets.shape, jnp.int32),
            pltpu.VMEM(measured.shape, f32),
            pltpu.SemaphoreType.DMA((2,)),
        ],
        compiler_params=params(),
        name="power",
    )(*map(in_hbm, (offsets, measured)), coef, near_probe, own)
    left_root = lax.ppermute(left, "tile", ring)
    message = shape((length + half_rows, length), f32)
    psi, far, pair_edge, *messages = pl.pallas_call(
        lambda *refs: forward_kernel(count, *refs),
        out_shape=(shape(probe.shape, f32), field, square) + (message,) * count,
        in_specs=[VM] * 8,
        out_specs=(VM,) * (3 + count),
        scratch_shapes=[
            pltpu.VMEM((materials, half, length), f32),
            pltpu.VMEM((length, length), f32),
        ],
        compiler_params=params(),
        name="forward",
    )(near, halo, near_probe, table, coef, power, total_edge, other_edge)
    shares = [messages[0]]
    for k in range(1, count):
        shares.append(lax.ppermute(messages[k], "wave", [(w, w ^ k) for w in range(count)]))
    edges = [pair_edge] + [among_last(pair_edge, k) for k in range(2, count, 2)]

    *sends, scale = pl.pallas_call(
        lambda *refs: backward_kernel(tiles, count, *refs),
        out_shape=(share,) * count + (shape((half_rows, length), f32),),
        in_specs=[VM] * (7 + count + len(edges)),
        out_specs=(VM,) * (count + 1),
        scratch_shapes=[
            pltpu.VMEM((2 * length, length), f32),
            pltpu.VMEM((materials, length, length), f32),
            pltpu.VMEM((length, 2 * length), f32),
        ],
        compiler_params=params(),
        name="backward",
    )(right_root, left_root, table, coef, psi, far, far_edge, *shares, *edges)

    def owner(t, q):
        return (t + (q >= count // 2)) % tiles * count + q

    arrived = []
    for k in range(count):
        pairs = [(t * count + w, owner(t, w ^ k)) for t in range(tiles) for w in range(count)]
        arrived.append(lax.ppermute(sends[k], both, [p for p in pairs if p[0] != p[1]]))

    new = pl.pallas_call(
        lambda *refs: update_kernel(count, *refs),
        out_shape=share,
        in_specs=[VM] * (3 + count),
        out_specs=VM,
        compiler_params=params(),
        name="update",
    )(here, scale, sends[0], *arrived)

    parts = [new]
    for k in range(1, count):
        parts.append(lax.ppermute(new, "wave", [(w, w ^ k) for w in range(count)]))
    return pl.pallas_call(
        lambda *refs: join_kernel(count, *refs),
        out_shape=shape((materials, length, length), f32),
        in_specs=[VM] * count,
        out_specs=VM,
        compiler_params=params(),
        name="join",
    )(*parts)


def solution(mesh):
    in_specs = (
        P(None, None, "tile"),
        P("tile", None, None),
        P("tile"),
        P("wave", None, None, None),
        P("wave"),
        P("wave"),
        P("wave", None),
        P(),
    )
    out_specs = P(None, None, "tile")
    tiles, count = mesh.shape["tile"], mesh.shape["wave"]
    return jax.shard_map(
        lambda *args: per_device(tiles, count, *args),
        mesh=mesh,
        in_specs=in_specs,
        out_specs=out_specs,
        check_vma=False,
    )
```

```python
import math

import jax
import jax.numpy as jnp
import numpy as np
from jax import lax
from jax.experimental import pallas as pl
from jax.experimental.pallas import tpu as pltpu
from jax.sharding import PartitionSpec as P

WAVES = 48

relax = 4.0
floor_level = 1.0

UNROLL = 12
EDGE_UNROLL = 12
CHUNK = 32

VM = pl.BlockSpec(memory_space=pltpu.VMEM)
ANY = pl.BlockSpec(memory_space=pltpu.HBM)
f32 = jnp.float32
bf16 = jnp.bfloat16


def fit(parity, degree):
    nodes = 0.5 * np.cos(np.pi * (np.arange(400) + 0.5) / 800)
    turns = 2 * np.pi * nodes
    value = np.sin(turns) if parity else np.cos(turns)
    powers = np.stack([nodes ** (parity + 2 * i) for i in range(degree)], axis=1)
    return [float(c) for c in np.linalg.lstsq(powers, value, rcond=None)[0]]


SIN = fit(1, 6)
COS = fit(0, 7)


def horner(square, coefs):
    total = coefs[-1]
    for c in coefs[-2::-1]:
        total = total * square + c
    return total


def cos_sin(turns):
    r = turns - jnp.round(turns)
    square = r * r
    return horner(square, COS), horner(square, SIN) * r


def lanes(rows, length):
    return lax.broadcasted_iota(jnp.int32, (rows, length), 1)


def halves_packed(top, bottom, upper):
    length = top.shape[-1]
    half = length // 2
    low = lanes(top.shape[0], length) < half
    if upper:
        return jnp.where(low, pltpu.roll(top, half, 1), bottom)
    return jnp.where(low, top, pltpu.roll(bottom, half, 1))


def block(table_ref, s, kind):
    re, im, neg = table_ref[s, 0], table_ref[s, 1], table_ref[s, 2]
    top, bottom = ((re, neg), (im, re)) if kind == "L" else ((re, im), (neg, re))
    return jnp.concatenate(
        [jnp.concatenate(top, axis=1), jnp.concatenate(bottom, axis=1)], axis=0
    )


def piece(array, q, count, half_rows):
    groups = count // 2
    rows = 2 * half_rows
    start = pl.multiple_of(lax.rem(q, groups) * rows, half_rows)
    top = array[pl.ds(start, half_rows), :]
    bottom = array[pl.ds(start + half_rows, half_rows), :]
    return jnp.where(
        q < groups, halves_packed(top, bottom, False), halves_packed(top, bottom, True)
    )


def first_kernel(
    spectrum_any, wave_any, edge_any, band_any, maps_any, probe_any,
    table, coef, probe, near, own, far_edge, total_edge,
    spectrum, wave_index, edge_band, band_coef, maps, packed, sems,
):
    copies = [
        pltpu.make_async_copy(source, target, sems.at[i])
        for i, (source, target) in enumerate(
            (
                (wave_any, wave_index),
                (edge_any, edge_band),
                (band_any, band_coef),
                (spectrum_any, spectrum),
                (maps_any, maps),
                (probe_any, probe),
            )
        )
    ]
    for copy in copies:
        copy.start()
    materials, length, _ = maps.shape
    half = length // 2
    slots = probe.shape[0]
    group = 8
    centred_lane = (lanes(group, length) - half).astype(f32)
    row = lax.broadcasted_iota(jnp.int32, (group, length), 0)
    fine = row.astype(f32) * centred_lane / length
    normaliser = 1.0 / math.sqrt(length)
    coarse_rows = length // group
    copies[0].wait()

    def tables(s, carry):
        which = jnp.full((group, length), wave_index[s], jnp.int32).astype(f32)
        sampling = 0.6 + 0.4 * which / (WAVES - 1)
        fine_cos, fine_sin = cos_sin(sampling * fine)
        fine_cos, fine_sin = fine_cos * normaliser, fine_sin * normaliser
        for base in range(0, coarse_rows, group):
            step = ((row + base) * group - half).astype(f32) * centred_lane / length
            cos, sin = cos_sin(sampling * step)
            for i in range(0, group, 2):
                parts = []
                for j in (i, i + 1):
                    c = jnp.broadcast_to(cos[j : j + 1], (group, length))
                    n = jnp.broadcast_to(sin[j : j + 1], (group, length))
                    parts.append((c * fine_cos - n * fine_sin, n * fine_cos + c * fine_sin))
                at = pl.ds((base + i) * group, 2 * group)
                re = jnp.concatenate([parts[0][0], parts[1][0]], axis=0).astype(bf16)
                positive = jnp.concatenate([parts[0][1], parts[1][1]], axis=0)
                table[s, 0, at, :] = re
                table[s, 1, at, :] = (-positive).astype(bf16)
                table[s, 2, at, :] = positive.astype(bf16)
        return carry

    lax.fori_loop(0, slots, tables, 0, unroll=6)

    for copy in copies[1:]:
        copy.wait()
    for s in range(slots):
        for m in range(materials):
            band = edge_band[m, s]
            a, b = band_coef[band, 0, m], band_coef[band, 1, m]
            coef[s, m, :] = jnp.full((length,), a * (-math.log2(math.e)), f32)
            coef[s, materials + m, :] = jnp.full((length,), b * (0.5 / math.pi), f32)
            coef[s, 2 * materials + m, :] = jnp.full((length,), a, f32)
            coef[s, 3 * materials + m, :] = jnp.full((length,), b, f32)
        coef[s, 4 * materials, :] = jnp.full((length,), spectrum[s], f32)
    for m in range(materials):
        own[m] = pltpu.roll(maps[m], half, 1)
        packed[m] = halves_packed(own[m, :half], own[m, half:], False)

    def near_object(s, carry):
        for start in range(0, half, CHUNK):
            parts = object_of(coef, s, [packed[m, start : start + CHUNK] for m in range(materials)])
            for i, part in enumerate(parts):
                near[s, i, start : start + CHUNK] = part
                near[s, i, half + start : half + start + CHUNK] = pltpu.roll(part, half, 1)
        return carry

    lax.fori_loop(0, slots, near_object, 0, unroll=6)

    @pl.when(lax.axis_index("tile") == lax.axis_size("tile") - 1)
    def _():
        total_edge[...] = jnp.zeros_like(total_edge)
        low = lanes(length, length) < half

        def step(s, carry):
            re, im, cos, sin = probe[s, 0], probe[s, 1], near[s, 0], near[s, 1]
            field = [
                (jnp.where(low, re * cos - im * sin, re), jnp.where(low, re * sin + im * cos, im))
            ]
            got = transform(block(table, s, "L"), block(table, s, "R"), field)
            far_edge[s] = got
            re, im = got[:, :length], got[:, length:]
            total_edge[...] += coef[s, 4 * materials : 4 * materials + 1] * (re * re + im * im)
            return carry

        lax.fori_loop(0, slots, step, 0, unroll=EDGE_UNROLL)


def power_kernel(
    count, offsets_any, measured_any, coef, probe, own,
    here, power, left_root, right_root,
    offsets, measured, sems,
):
    copies = [
        pltpu.make_async_copy(source, target, sems.at[i])
        for i, (source, target) in enumerate(((offsets_any, offsets), (measured_any, measured)))
    ]
    for copy in copies:
        copy.start()
    materials, length, _ = own.shape
    half = length // 2
    slots = probe.shape[0]
    tile, tiles = lax.axis_index("tile"), lax.axis_size("tile")
    me = lax.axis_index("wave")
    low = lanes(CHUNK, length) < half
    frames = jnp.where(
        low,
        jnp.where(tile == tiles - 1, 1.0, 2.0),
        jnp.where(tile == 0, 1.0, 2.0),
    )
    for start in range(0, length, CHUNK):
        at = slice(start, start + CHUNK)
        window = [own[m, at] for m in range(materials)]

        def add(s, total):
            absorb = None
            for m in range(materials):
                term = coef[s, m : m + 1] * window[m]
                absorb = term if absorb is None else absorb + term
            re, im = probe[s, 0, at], probe[s, 1, at]
            weight = coef[s, 4 * materials : 4 * materials + 1]
            return total + (weight * jnp.exp2(absorb + absorb)) * (re * re + im * im)

        total = lax.fori_loop(0, slots, add, jnp.zeros((CHUNK, length), f32), unroll=4)
        power[at] = frames * total
    half_rows = length // count
    for m in range(materials):
        here[m] = piece(own.at[m], me, count, half_rows)
    for copy in copies:
        copy.wait()
    left_first = offsets[0] < offsets[1]
    first, second = jnp.sqrt(measured[0]), jnp.sqrt(measured[1])
    left_root[...] = jnp.where(left_first, first, second)
    right_root[...] = jnp.where(left_first, second, first)


def object_of(coef, s, window):
    materials = len(window)
    absorb, phase = None, None
    for m, w in enumerate(window):
        a = coef[s, m : m + 1] * w
        b = coef[s, materials + m : materials + m + 1] * w
        absorb = a if absorb is None else absorb + a
        phase = b if phase is None else phase + b
    damping = jnp.exp2(absorb)
    cos, sin = cos_sin(phase)
    return damping * cos, damping * sin


def transform(left, right, fields):
    length = fields[0][0].shape[0]
    stacked = jnp.concatenate(
        [jnp.concatenate([re.astype(bf16), im.astype(bf16)], axis=0) for re, im in fields], axis=1
    )
    mid = jnp.dot(left, stacked, preferred_element_type=f32).astype(bf16)
    beside = jnp.concatenate(
        [
            jnp.concatenate(
                [mid[:length, i * length : (i + 1) * length], mid[length:, i * length : (i + 1) * length]], axis=1
            )
            for i in range(len(fields))
        ],
        axis=0,
    )
    if len(fields) == 1:
        beside = jnp.concatenate([beside, beside], axis=0)
    return jnp.dot(beside, right, preferred_element_type=f32)[: len(fields) * length]


def forward_kernel(count, near, halo, probe, table, coef, power, psi, far, *rest):
    messages, (beyond, total) = rest[:count], rest[count:]
    materials, length, _ = halo.shape
    half = length // 2
    slots = probe.shape[0]
    me = lax.axis_index("wave")
    for m in range(materials):
        beyond[m] = halves_packed(halo[m, :half], halo[m, half:], False)
    total[...] = jnp.zeros_like(total)
    low = lanes(CHUNK, length) < half

    def exit_wave(s):
        for start in range(0, half, CHUNK):
            parts = object_of(coef, s, [beyond[m, start : start + CHUNK] for m in range(materials)])
            upper, lower = slice(start, start + CHUNK), slice(half + start, half + start + CHUNK)
            for at, turned in ((upper, True), (lower, False)):
                cos, sin = [
                    jnp.where(low, near[s, i, at], pltpu.roll(part, half, 1) if turned else part)
                    for i, part in enumerate(parts)
                ]
                re, im = probe[s, 0, at], probe[s, 1, at]
                psi[s, 0, at] = re * cos - im * sin
                psi[s, 1, at] = re * sin + im * cos

    def step(s, joined):
        exit_wave(s)
        re, im = psi[s, 0], psi[s, 1]
        if joined:
            low = lanes(length, length) < half
            re, im = jnp.where(low, probe[s, 0], re), jnp.where(low, probe[s, 1], im)
        got = transform(block(table, s, "L"), block(table, s, "R"), [(re, im)])
        far[s] = got
        re, im = got[:, :length], got[:, length:]
        total[...] += coef[s, 4 * materials : 4 * materials + 1] * (re * re + im * im)

    edge = lax.axis_index("tile") == lax.axis_size("tile") - 1

    for joined in (False, True):

        @pl.when(edge == joined)
        def _():
            lax.fori_loop(
                0, slots, lambda s, c: (step(s, joined), c)[1], 0, unroll=EDGE_UNROLL if joined else UNROLL
            )

    half_rows = length // count
    for k, message in enumerate(messages):
        message[:length] = total[...]
        message[length:] = piece(power, jnp.bitwise_xor(me, k), count, half_rows)


def add_kernel(one, other, _, out):
    out[...] = one[...] + other[...]


def backward_kernel(tiles, count, right_root, left_root, table, coef, psi, far, far_edge, *rest):
    shares, rest = rest[:count], rest[count:]
    edges, rest = rest[: count // 2], rest[count // 2 :]
    sends, rest = rest[:count], rest[count:]
    scale, shortfall, gradient, back = rest
    length = right_root.shape[0]
    materials = gradient.shape[0]
    half = length // 2
    slots = psi.shape[0]
    edge = lax.axis_index("tile") == tiles - 1
    me = lax.axis_index("wave")
    half_rows = length // count
    powers = shares[0][length:]
    for share in shares[1:]:
        powers = powers + share[length:]
    scale[...] = relax / (powers + 1.0)
    gradient[...] = jnp.zeros_like(gradient)

    def inverse(shares):
        intensity = shares[0][:length]
        for share in shares[1:]:
            intensity = intensity + share[:length]
        return lax.rsqrt(jnp.maximum(intensity, floor_level))

    def delta(s, far, at):
        factor = coef[s, 4 * materials : 4 * materials + 1] * shortfall[at : at + length]
        return factor * far[s, :, :length], factor * far[s, :, length:]

    def collect(s):
        for start in range(0, length, CHUNK):
            at = slice(start, start + CHUNK)
            re, im = psi[s, 0, at], psi[s, 1, at]
            back_re, back_im = back[at, :length], back[at, length:]
            cross_re = re * back_re + im * back_im
            cross_im = re * back_im - im * back_re
            for m in range(materials):
                a = coef[s, 2 * materials + m : 2 * materials + m + 1]
                b = coef[s, 3 * materials + m : 3 * materials + m + 1]
                gradient[m, at] += b * cross_im - a * cross_re

    @pl.when(jnp.logical_not(edge))
    def _():
        shortfall[:length] = (right_root[...] + left_root[...]) * inverse(shares) - 2.0

        def step(s, carry):
            back[...] = transform(block(table, s, "R"), block(table, s, "L"), [delta(s, far, 0)])
            collect(s)
            return carry

        lax.fori_loop(0, slots, step, 0, unroll=UNROLL)

    @pl.when(edge)
    def _():
        shortfall[:length] = left_root[...] * inverse(shares) - 1.0
        shortfall[length:] = right_root[...] * inverse(edges) - 1.0
        low = (lax.broadcasted_iota(jnp.int32, (length, 2 * length), 1) & (length - 1)) < half

        def step(s, carry):
            both = transform(
                block(table, s, "R"), block(table, s, "L"), [delta(s, far, 0), delta(s, far_edge, length)]
            )
            back[...] = jnp.where(low, both[length:], both[:length])
            collect(s)
            return carry

        lax.fori_loop(0, slots, step, 0, unroll=EDGE_UNROLL)

    for k, send in enumerate(sends):
        for m in range(materials):
            send[m] = piece(gradient.at[m], jnp.bitwise_xor(me, k), count, half_rows)


def update_kernel(count, here, scale, *refs):
    own, arrived, out = refs[0], refs[1:-1], refs[-1]
    me = lax.axis_index("wave")
    for m in range(here.shape[0]):
        total = jnp.where(me < count // 2, own[m], arrived[0][m])
        for other in arrived[1:]:
            total = total + other[m]
        out[m] = here[m] + scale[...] * total


def join_kernel(count, *refs):
    shares, out = refs[:count], refs[count]
    materials, length, _ = out.shape
    half = length // 2
    me = lax.axis_index("wave")
    half_rows = length // count
    groups = count // 2
    low = lanes(half_rows, length) < half
    for position in range(count):

        @pl.when(me == position)
        def _():
            held = lambda q: shares[q ^ position]
            for g in range(groups):
                right, left = held(g), held(g + groups)
                start = g * 2 * half_rows
                for m in range(materials):
                    r, l = right[m], left[m]
                    out[m, start : start + half_rows] = jnp.where(low, l, pltpu.roll(r, half, 1))
                    out[m, start + half_rows : start + 2 * half_rows] = jnp.where(
                        low, pltpu.roll(l, half, 1), r
                    )


def in_hbm(array):
    return pltpu.with_memory_space_constraint(array, pltpu.HBM)


def params(mib=40):
    return pltpu.CompilerParams(vmem_limit_bytes=mib * 2**20)


def per_device(tiles, count, maps, measured, offsets, probe, spectrum, wave_index, edge_band, band_coef):
    materials, length, columns = maps.shape
    slots = probe.shape[0]
    half = length // 2
    shape = jax.ShapeDtypeStruct
    half_rows = length // count
    partners = [count // 2] + [k for k in range(1, count) if k != count // 2]
    square = shape((length, length), f32)
    share = shape((materials, half_rows, length), f32)

    ring = [(i, (i - 1) % tiles) for i in range(tiles)]
    halo = lax.ppermute(maps, "tile", ring)

    band_first = jnp.transpose(band_coef, (1, 0, 2))
    field = shape((slots, length, 2 * length), f32)
    table, coef, near_probe, near, own, far_edge, total_edge = pl.pallas_call(
        first_kernel,
        out_shape=(
            shape((slots, 3, length, length), bf16),
            shape((slots, 6 * materials, length), f32),
            shape(probe.shape, f32),
            shape(probe.shape, f32),
            shape(maps.shape, f32),
            field,
            square,
        ),
        in_specs=[ANY] * 6,
        out_specs=(VM,) * 7,
        scratch_shapes=[
            pltpu.SMEM(spectrum.shape, f32),
            pltpu.SMEM(wave_index.shape, jnp.int32),
            pltpu.SMEM(edge_band.shape[::-1], jnp.int32),
            pltpu.SMEM(band_first.shape, f32),
            pltpu.VMEM(maps.shape, f32),
            pltpu.VMEM((materials, half, length), f32),
            pltpu.SemaphoreType.DMA((6,)),
        ],
        compiler_params=params(),
        cost_estimate=pl.CostEstimate(flops=10**9, bytes_accessed=2**22, transcendentals=0),
        name="tables",
    )(*map(in_hbm, (spectrum, wave_index, edge_band.T, band_first, maps, probe)))
    both = ("tile", "wave")
    last = (tiles - 1) * count

    def among_last(array, k):
        return lax.ppermute(array, both, [(last + w, last + (w ^ k)) for w in range(count)])

    other_edge = among_last(total_edge, 1)
    here, power, left, right_root = pl.pallas_call(
        lambda *refs: power_kernel(count, *refs),
        out_shape=(share, square, square, square),
        in_specs=[ANY] * 2 + [VM] * 3,
        out_specs=(VM,) * 4,
        scratch_shapes=[
            pltpu.SMEM(offsets.shape, jnp.int32),
            pltpu.VMEM(measured.shape, f32),
            pltpu.SemaphoreType.DMA((2,)),
        ],
        compiler_params=params(),
        name="power",
    )(*map(in_hbm, (offsets, measured)), coef, near_probe, own)
    left_root = lax.ppermute(left, "tile", ring)
    message = shape((length + half_rows, length), f32)
    psi, far, *messages = pl.pallas_call(
        lambda *refs: forward_kernel(count, *refs),
        out_shape=(shape(probe.shape, f32), field) + (message,) * count,
        in_specs=[VM] * 6,
        out_specs=(VM,) * (2 + count),
        scratch_shapes=[
            pltpu.VMEM((materials, half, length), f32),
            pltpu.VMEM((length, length), f32),
        ],
        compiler_params=params(),
        name="forward",
    )(near, halo, near_probe, table, coef, power)
    shares = [messages[0]]
    for k in partners:
        shares.append(lax.ppermute(messages[k], "wave", [(w, w ^ k) for w in range(count)]))
    pair_edge = pl.pallas_call(
        add_kernel,
        out_shape=square,
        in_specs=[VM] * 3,
        out_specs=VM,
        compiler_params=params(),
        name="pair",
    )(total_edge, other_edge, messages[0])
    edges = [pair_edge] + [among_last(pair_edge, k) for k in range(2, count, 2)]

    *sends, scale = pl.pallas_call(
        lambda *refs: backward_kernel(tiles, count, *refs),
        out_shape=(share,) * count + (shape((half_rows, length), f32),),
        in_specs=[VM] * (7 + count + len(edges)),
        out_specs=(VM,) * (count + 1),
        scratch_shapes=[
            pltpu.VMEM((2 * length, length), f32),
            pltpu.VMEM((materials, length, length), f32),
            pltpu.VMEM((length, 2 * length), f32),
        ],
        compiler_params=params(),
        name="backward",
    )(right_root, left_root, table, coef, psi, far, far_edge, *shares, *edges)

    def owner(t, q):
        return (t + (q >= count // 2)) % tiles * count + q

    arrived = []
    for k in (0, *partners):
        pairs = [(t * count + w, owner(t, w ^ k)) for t in range(tiles) for w in range(count)]
        arrived.append(lax.ppermute(sends[k], both, [p for p in pairs if p[0] != p[1]]))

    new = pl.pallas_call(
        lambda *refs: update_kernel(count, *refs),
        out_shape=share,
        in_specs=[VM] * (3 + count),
        out_specs=VM,
        compiler_params=params(),
        name="update",
    )(here, scale, sends[0], *arrived)

    parts = [new]
    for k in range(1, count):
        parts.append(lax.ppermute(new, "wave", [(w, w ^ k) for w in range(count)]))
    return pl.pallas_call(
        lambda *refs: join_kernel(count, *refs),
        out_shape=shape((materials, length, length), f32),
        in_specs=[VM] * count,
        out_specs=VM,
        compiler_params=params(),
        name="join",
    )(*parts)


def solution(mesh):
    in_specs = (
        P(None, None, "tile"),
        P("tile", None, None),
        P("tile"),
        P("wave", None, None, None),
        P("wave"),
        P("wave"),
        P("wave", None),
        P(),
    )
    out_specs = P(None, None, "tile")
    tiles, count = mesh.shape["tile"], mesh.shape["wave"]
    return jax.shard_map(
        lambda *args: per_device(tiles, count, *args),
        mesh=mesh,
        in_specs=in_specs,
        out_specs=out_specs,
        check_vma=False,
    )
```

```python
import math

import jax
import jax.numpy as jnp
import numpy as np
from jax import lax
from jax.experimental import pallas as pl
from jax.experimental.pallas import tpu as pltpu
from jax.sharding import PartitionSpec as P

WAVES = 48

relax = 4.0
floor_level = 1.0

UNROLL = 12
EDGE_UNROLL = 12
CHUNK = 32

VM = pl.BlockSpec(memory_space=pltpu.VMEM)
ANY = pl.BlockSpec(memory_space=pltpu.HBM)
f32 = jnp.float32
bf16 = jnp.bfloat16


def fit(parity, degree):
    nodes = 0.5 * np.cos(np.pi * (np.arange(400) + 0.5) / 800)
    turns = 2 * np.pi * nodes
    value = np.sin(turns) if parity else np.cos(turns)
    powers = np.stack([nodes ** (parity + 2 * i) for i in range(degree)], axis=1)
    return [float(c) for c in np.linalg.lstsq(powers, value, rcond=None)[0]]


SIN = fit(1, 6)
COS = fit(0, 7)


def horner(square, coefs):
    total = coefs[-1]
    for c in coefs[-2::-1]:
        total = total * square + c
    return total


def cos_sin(turns):
    r = turns - jnp.round(turns)
    square = r * r
    return horner(square, COS), horner(square, SIN) * r


def lanes(rows, length):
    return lax.broadcasted_iota(jnp.int32, (rows, length), 1)


def halves_packed(top, bottom, upper):
    length = top.shape[-1]
    half = length // 2
    low = lanes(top.shape[0], length) < half
    if upper:
        return jnp.where(low, pltpu.roll(top, half, 1), bottom)
    return jnp.where(low, top, pltpu.roll(bottom, half, 1))


def block(table_ref, s, kind):
    re, im, neg = table_ref[s, 0], table_ref[s, 1], table_ref[s, 2]
    top, bottom = ((re, neg), (im, re)) if kind == "L" else ((re, im), (neg, re))
    return jnp.concatenate(
        [jnp.concatenate(top, axis=1), jnp.concatenate(bottom, axis=1)], axis=0
    )


def piece(array, q, count, half_rows):
    groups = count // 2
    rows = 2 * half_rows
    start = pl.multiple_of(lax.rem(q, groups) * rows, half_rows)
    top = array[pl.ds(start, half_rows), :]
    bottom = array[pl.ds(start + half_rows, half_rows), :]
    return jnp.where(
        q < groups, halves_packed(top, bottom, False), halves_packed(top, bottom, True)
    )


def first_kernel(
    spectrum_any, wave_any, edge_any, band_any, maps_any, probe_any, offsets_any, measured_any,
    table, coef, probe, near, own, far_edge, total_edge, left_root, right_root,
    spectrum, wave_index, edge_band, band_coef, maps, packed, offsets, measured, sems,
):
    copies = [
        pltpu.make_async_copy(source, target, sems.at[i])
        for i, (source, target) in enumerate(
            (
                (wave_any, wave_index),
                (edge_any, edge_band),
                (band_any, band_coef),
                (spectrum_any, spectrum),
                (maps_any, maps),
                (probe_any, probe),
                (offsets_any, offsets),
                (measured_any, measured),
            )
        )
    ]
    for copy in copies:
        copy.start()
    materials, length, _ = maps.shape
    half = length // 2
    slots = probe.shape[0]
    group = 8
    centred_lane = (lanes(group, length) - half).astype(f32)
    row = lax.broadcasted_iota(jnp.int32, (group, length), 0)
    fine = row.astype(f32) * centred_lane / length
    normaliser = 1.0 / math.sqrt(length)
    coarse_rows = length // group
    copies[0].wait()

    def tables(s, carry):
        which = jnp.full((group, length), wave_index[s], jnp.int32).astype(f32)
        sampling = 0.6 + 0.4 * which / (WAVES - 1)
        fine_cos, fine_sin = cos_sin(sampling * fine)
        fine_cos, fine_sin = fine_cos * normaliser, fine_sin * normaliser
        for base in range(0, coarse_rows, group):
            step = ((row + base) * group - half).astype(f32) * centred_lane / length
            cos, sin = cos_sin(sampling * step)
            for i in range(0, group, 2):
                parts = []
                for j in (i, i + 1):
                    c = jnp.broadcast_to(cos[j : j + 1], (group, length))
                    n = jnp.broadcast_to(sin[j : j + 1], (group, length))
                    parts.append((c * fine_cos - n * fine_sin, n * fine_cos + c * fine_sin))
                at = pl.ds((base + i) * group, 2 * group)
                re = jnp.concatenate([parts[0][0], parts[1][0]], axis=0).astype(bf16)
                positive = jnp.concatenate([parts[0][1], parts[1][1]], axis=0)
                table[s, 0, at, :] = re
                table[s, 1, at, :] = (-positive).astype(bf16)
                table[s, 2, at, :] = positive.astype(bf16)
        return carry

    lax.fori_loop(0, slots, tables, 0, unroll=6)

    for copy in copies[1:]:
        copy.wait()
    for s in range(slots):
        for m in range(materials):
            band = edge_band[m, s]
            a, b = band_coef[band, 0, m], band_coef[band, 1, m]
            coef[s, m, :] = jnp.full((length,), a * (-math.log2(math.e)), f32)
            coef[s, materials + m, :] = jnp.full((length,), b * (0.5 / math.pi), f32)
            coef[s, 2 * materials + m, :] = jnp.full((length,), a, f32)
            coef[s, 3 * materials + m, :] = jnp.full((length,), b, f32)
        coef[s, 4 * materials, :] = jnp.full((length,), spectrum[s], f32)
    left_first = offsets[0] < offsets[1]
    first, second = jnp.sqrt(measured[0]), jnp.sqrt(measured[1])
    left_root[...] = jnp.where(left_first, first, second)
    right_root[...] = jnp.where(left_first, second, first)
    for m in range(materials):
        own[m] = pltpu.roll(maps[m], half, 1)
        packed[m] = halves_packed(own[m, :half], own[m, half:], False)

    def near_object(s, carry):
        for start in range(0, half, CHUNK):
            parts = object_of(coef, s, [packed[m, start : start + CHUNK] for m in range(materials)])
            for i, part in enumerate(parts):
                near[s, i, start : start + CHUNK] = part
                near[s, i, half + start : half + start + CHUNK] = pltpu.roll(part, half, 1)
        return carry

    lax.fori_loop(0, slots, near_object, 0, unroll=6)

    @pl.when(lax.axis_index("tile") == lax.axis_size("tile") - 1)
    def _():
        total_edge[...] = jnp.zeros_like(total_edge)
        low = lanes(length, length) < half

        def step(s, carry):
            re, im, cos, sin = probe[s, 0], probe[s, 1], near[s, 0], near[s, 1]
            field = [
                (jnp.where(low, re * cos - im * sin, re), jnp.where(low, re * sin + im * cos, im))
            ]
            got = transform(block(table, s, "L"), block(table, s, "R"), field)
            far_edge[s] = got
            re, im = got[:, :length], got[:, length:]
            total_edge[...] += coef[s, 4 * materials : 4 * materials + 1] * (re * re + im * im)
            return carry

        lax.fori_loop(0, slots, step, 0, unroll=EDGE_UNROLL)


def power_kernel(count, coef, probe, own, left_root, here, power, left_out):
    left_out[...] = left_root[...]
    materials, length, _ = own.shape
    half = length // 2
    slots = probe.shape[0]
    tile, tiles = lax.axis_index("tile"), lax.axis_size("tile")
    me = lax.axis_index("wave")
    low = lanes(CHUNK, length) < half
    frames = jnp.where(
        low,
        jnp.where(tile == tiles - 1, 1.0, 2.0),
        jnp.where(tile == 0, 1.0, 2.0),
    )
    for start in range(0, length, CHUNK):
        at = slice(start, start + CHUNK)
        window = [own[m, at] for m in range(materials)]

        def add(s, total):
            absorb = None
            for m in range(materials):
                term = coef[s, m : m + 1] * window[m]
                absorb = term if absorb is None else absorb + term
            re, im = probe[s, 0, at], probe[s, 1, at]
            weight = coef[s, 4 * materials : 4 * materials + 1]
            return total + (weight * jnp.exp2(absorb + absorb)) * (re * re + im * im)

        total = lax.fori_loop(0, slots, add, jnp.zeros((CHUNK, length), f32), unroll=UNROLL)
        power[at] = frames * total
    half_rows = length // count
    for m in range(materials):
        here[m] = piece(own.at[m], me, count, half_rows)


def object_of(coef, s, window):
    materials = len(window)
    absorb, phase = None, None
    for m, w in enumerate(window):
        a = coef[s, m : m + 1] * w
        b = coef[s, materials + m : materials + m + 1] * w
        absorb = a if absorb is None else absorb + a
        phase = b if phase is None else phase + b
    damping = jnp.exp2(absorb)
    cos, sin = cos_sin(phase)
    return damping * cos, damping * sin


def transform(left, right, fields):
    length = fields[0][0].shape[0]
    stacked = jnp.concatenate(
        [jnp.concatenate([re.astype(bf16), im.astype(bf16)], axis=0) for re, im in fields], axis=1
    )
    mid = jnp.dot(left, stacked, preferred_element_type=f32).astype(bf16)
    beside = jnp.concatenate(
        [
            jnp.concatenate(
                [mid[:length, i * length : (i + 1) * length], mid[length:, i * length : (i + 1) * length]], axis=1
            )
            for i in range(len(fields))
        ],
        axis=0,
    )
    if len(fields) == 1:
        beside = jnp.concatenate([beside, beside], axis=0)
    return jnp.dot(beside, right, preferred_element_type=f32)[: len(fields) * length]


def forward_kernel(count, near, halo, probe, table, coef, power, psi, far, *rest):
    messages, (beyond, total) = rest[:count], rest[count:]
    materials, length, _ = halo.shape
    half = length // 2
    slots = probe.shape[0]
    me = lax.axis_index("wave")
    for m in range(materials):
        beyond[m] = halves_packed(halo[m, :half], halo[m, half:], False)
    total[...] = jnp.zeros_like(total)
    low = lanes(CHUNK, length) < half

    def exit_wave(s):
        for start in range(0, half, CHUNK):
            parts = object_of(coef, s, [beyond[m, start : start + CHUNK] for m in range(materials)])
            upper, lower = slice(start, start + CHUNK), slice(half + start, half + start + CHUNK)
            for at, turned in ((upper, True), (lower, False)):
                cos, sin = [
                    jnp.where(low, near[s, i, at], pltpu.roll(part, half, 1) if turned else part)
                    for i, part in enumerate(parts)
                ]
                re, im = probe[s, 0, at], probe[s, 1, at]
                psi[s, 0, at] = re * cos - im * sin
                psi[s, 1, at] = re * sin + im * cos

    def step(s, joined):
        exit_wave(s)
        re, im = psi[s, 0], psi[s, 1]
        if joined:
            low = lanes(length, length) < half
            re, im = jnp.where(low, probe[s, 0], re), jnp.where(low, probe[s, 1], im)
        got = transform(block(table, s, "L"), block(table, s, "R"), [(re, im)])
        far[s] = got
        re, im = got[:, :length], got[:, length:]
        total[...] += coef[s, 4 * materials : 4 * materials + 1] * (re * re + im * im)

    edge = lax.axis_index("tile") == lax.axis_size("tile") - 1

    for joined in (False, True):

        @pl.when(edge == joined)
        def _():
            lax.fori_loop(
                0, slots, lambda s, c: (step(s, joined), c)[1], 0, unroll=EDGE_UNROLL if joined else UNROLL
            )

    half_rows = length // count
    for k, message in enumerate(messages):
        message[:length] = total[...]
        message[length:] = piece(power, jnp.bitwise_xor(me, k), count, half_rows)


def add_kernel(one, other, _, out):
    out[...] = one[...] + other[...]


def backward_kernel(tiles, count, right_root, left_root, table, coef, psi, far, far_edge, *rest):
    shares, rest = rest[:count], rest[count:]
    edges, rest = rest[: count // 2], rest[count // 2 :]
    sends, rest = rest[:count], rest[count:]
    scale, shortfall, gradient, back = rest
    length = right_root.shape[0]
    materials = gradient.shape[0]
    half = length // 2
    slots = psi.shape[0]
    edge = lax.axis_index("tile") == tiles - 1
    me = lax.axis_index("wave")
    half_rows = length // count
    powers = shares[0][length:]
    for share in shares[1:]:
        powers = powers + share[length:]
    scale[...] = relax / (powers + 1.0)
    gradient[...] = jnp.zeros_like(gradient)

    def inverse(shares):
        intensity = shares[0][:length]
        for share in shares[1:]:
            intensity = intensity + share[:length]
        return lax.rsqrt(jnp.maximum(intensity, floor_level))

    def delta(s, far, at):
        factor = coef[s, 4 * materials : 4 * materials + 1] * shortfall[at : at + length]
        return factor * far[s, :, :length], factor * far[s, :, length:]

    def collect(s):
        for start in range(0, length, CHUNK):
            at = slice(start, start + CHUNK)
            re, im = psi[s, 0, at], psi[s, 1, at]
            back_re, back_im = back[at, :length], back[at, length:]
            cross_re = re * back_re + im * back_im
            cross_im = re * back_im - im * back_re
            for m in range(materials):
                a = coef[s, 2 * materials + m : 2 * materials + m + 1]
                b = coef[s, 3 * materials + m : 3 * materials + m + 1]
                gradient[m, at] += b * cross_im - a * cross_re

    @pl.when(jnp.logical_not(edge))
    def _():
        shortfall[:length] = (right_root[...] + left_root[...]) * inverse(shares) - 2.0

        def step(s, carry):
            back[...] = transform(block(table, s, "R"), block(table, s, "L"), [delta(s, far, 0)])
            collect(s)
            return carry

        lax.fori_loop(0, slots, step, 0, unroll=UNROLL)

    @pl.when(edge)
    def _():
        shortfall[:length] = left_root[...] * inverse(shares) - 1.0
        shortfall[length:] = right_root[...] * inverse(edges) - 1.0
        low = (lax.broadcasted_iota(jnp.int32, (length, 2 * length), 1) & (length - 1)) < half

        def step(s, carry):
            both = transform(
                block(table, s, "R"), block(table, s, "L"), [delta(s, far, 0), delta(s, far_edge, length)]
            )
            back[...] = jnp.where(low, both[length:], both[:length])
            collect(s)
            return carry

        lax.fori_loop(0, slots, step, 0, unroll=EDGE_UNROLL)

    for k, send in enumerate(sends):
        for m in range(materials):
            send[m] = piece(gradient.at[m], jnp.bitwise_xor(me, k), count, half_rows)


def update_kernel(count, here, scale, *refs):
    own, arrived, out = refs[0], refs[1:-1], refs[-1]
    me = lax.axis_index("wave")
    for m in range(here.shape[0]):
        total = jnp.where(me < count // 2, own[m], arrived[0][m])
        for other in arrived[1:]:
            total = total + other[m]
        out[m] = here[m] + scale[...] * total


def join_kernel(count, *refs):
    shares, out = refs[:count], refs[count]
    materials, length, _ = out.shape
    half = length // 2
    me = lax.axis_index("wave")
    half_rows = length // count
    groups = count // 2
    low = lanes(half_rows, length) < half
    for position in range(count):

        @pl.when(me == position)
        def _():
            held = lambda q: shares[q ^ position]
            for g in range(groups):
                right, left = held(g), held(g + groups)
                start = g * 2 * half_rows
                for m in range(materials):
                    r, l = right[m], left[m]
                    out[m, start : start + half_rows] = jnp.where(low, l, pltpu.roll(r, half, 1))
                    out[m, start + half_rows : start + 2 * half_rows] = jnp.where(
                        low, pltpu.roll(l, half, 1), r
                    )


def in_hbm(array):
    return pltpu.with_memory_space_constraint(array, pltpu.HBM)


def params(mib=40):
    return pltpu.CompilerParams(vmem_limit_bytes=mib * 2**20)


def per_device(tiles, count, maps, measured, offsets, probe, spectrum, wave_index, edge_band, band_coef):
    materials, length, columns = maps.shape
    slots = probe.shape[0]
    half = length // 2
    shape = jax.ShapeDtypeStruct
    half_rows = length // count
    rest = [k for k in range(1, count) if k != count // 2]
    first_order, second_order = rest[::-1] + [count // 2], [count // 2] + rest
    square = shape((length, length), f32)
    share = shape((materials, half_rows, length), f32)

    ring = [(i, (i - 1) % tiles) for i in range(tiles)]
    halo = lax.ppermute(maps, "tile", ring)

    band_first = jnp.transpose(band_coef, (1, 0, 2))
    field = shape((slots, length, 2 * length), f32)
    table, coef, near_probe, near, own, far_edge, total_edge, left, right_root = pl.pallas_call(
        first_kernel,
        out_shape=(
            shape((slots, 3, length, length), bf16),
            shape((slots, 6 * materials, length), f32),
            shape(probe.shape, f32),
            shape(probe.shape, f32),
            shape(maps.shape, f32),
            field,
            square,
            square,
            square,
        ),
        in_specs=[ANY] * 8,
        out_specs=(VM,) * 9,
        scratch_shapes=[
            pltpu.SMEM(spectrum.shape, f32),
            pltpu.SMEM(wave_index.shape, jnp.int32),
            pltpu.SMEM(edge_band.shape[::-1], jnp.int32),
            pltpu.SMEM(band_first.shape, f32),
            pltpu.VMEM(maps.shape, f32),
            pltpu.VMEM((materials, half, length), f32),
            pltpu.SMEM(offsets.shape, jnp.int32),
            pltpu.VMEM(measured.shape, f32),
            pltpu.SemaphoreType.DMA((8,)),
        ],
        compiler_params=params(),
        cost_estimate=pl.CostEstimate(flops=10**9, bytes_accessed=2**22, transcendentals=0),
        name="tables",
    )(*map(in_hbm, (spectrum, wave_index, edge_band.T, band_first, maps, probe, offsets, measured)))
    both = ("tile", "wave")
    last = (tiles - 1) * count

    def among_last(array, k):
        return lax.ppermute(array, both, [(last + w, last + (w ^ k)) for w in range(count)])

    other_edge = among_last(total_edge, 1)
    here, power, left = pl.pallas_call(
        lambda *refs: power_kernel(count, *refs),
        out_shape=(share, square, square),
        in_specs=[VM] * 4,
        out_specs=(VM,) * 3,
        compiler_params=params(),
        name="power",
    )(coef, near_probe, own, left)
    left_root = lax.ppermute(left, "tile", ring)
    message = shape((length + half_rows, length), f32)
    psi, far, *messages = pl.pallas_call(
        lambda *refs: forward_kernel(count, *refs),
        out_shape=(shape(probe.shape, f32), field) + (message,) * count,
        in_specs=[VM] * 6,
        out_specs=(VM,) * (2 + count),
        scratch_shapes=[
            pltpu.VMEM((materials, half, length), f32),
            pltpu.VMEM((length, length), f32),
        ],
        compiler_params=params(),
        name="forward",
    )(near, halo, near_probe, table, coef, power)
    shares = [messages[0]]
    for k in first_order:
        shares.append(lax.ppermute(messages[k], "wave", [(w, w ^ k) for w in range(count)]))
    pair_edge = pl.pallas_call(
        add_kernel,
        out_shape=square,
        in_specs=[VM] * 3,
        out_specs=VM,
        compiler_params=params(),
        name="pair",
    )(total_edge, other_edge, messages[0])
    edges = [pair_edge] + [among_last(pair_edge, k) for k in range(2, count, 2)]

    *sends, scale = pl.pallas_call(
        lambda *refs: backward_kernel(tiles, count, *refs),
        out_shape=(share,) * count + (shape((half_rows, length), f32),),
        in_specs=[VM] * (7 + count + len(edges)),
        out_specs=(VM,) * (count + 1),
        scratch_shapes=[
            pltpu.VMEM((2 * length, length), f32),
            pltpu.VMEM((materials, length, length), f32),
            pltpu.VMEM((length, 2 * length), f32),
        ],
        compiler_params=params(),
        name="backward",
    )(right_root, left_root, table, coef, psi, far, far_edge, *shares, *edges)

    def owner(t, q):
        return (t + (q >= count // 2)) % tiles * count + q

    arrived = []
    for k in (0, *second_order):
        pairs = [(t * count + w, owner(t, w ^ k)) for t in range(tiles) for w in range(count)]
        arrived.append(lax.ppermute(sends[k], both, [p for p in pairs if p[0] != p[1]]))

    new = pl.pallas_call(
        lambda *refs: update_kernel(count, *refs),
        out_shape=share,
        in_specs=[VM] * (3 + count),
        out_specs=VM,
        compiler_params=params(),
        name="update",
    )(here, scale, sends[0], *arrived)

    parts = [new]
    for k in range(1, count):
        parts.append(lax.ppermute(new, "wave", [(w, w ^ k) for w in range(count)]))
    return pl.pallas_call(
        lambda *refs: join_kernel(count, *refs),
        out_shape=shape((materials, length, length), f32),
        in_specs=[VM] * count,
        out_specs=VM,
        compiler_params=params(),
        name="join",
    )(*parts)


def solution(mesh):
    in_specs = (
        P(None, None, "tile"),
        P("tile", None, None),
        P("tile"),
        P("wave", None, None, None),
        P("wave"),
        P("wave"),
        P("wave", None),
        P(),
    )
    out_specs = P(None, None, "tile")
    tiles, count = mesh.shape["tile"], mesh.shape["wave"]
    return jax.shard_map(
        lambda *args: per_device(tiles, count, *args),
        mesh=mesh,
        in_specs=in_specs,
        out_specs=out_specs,
        check_vma=False,
    )
```

```python
import math

import jax
import jax.numpy as jnp
import numpy as np
from jax import lax
from jax.experimental import pallas as pl
from jax.experimental.pallas import tpu as pltpu
from jax.sharding import PartitionSpec as P

WAVES = 48

relax = 4.0
floor_level = 1.0

UNROLL = 12
EDGE_UNROLL = 12
CHUNK = 32

VM = pl.BlockSpec(memory_space=pltpu.VMEM)
ANY = pl.BlockSpec(memory_space=pltpu.HBM)
f32 = jnp.float32
bf16 = jnp.bfloat16


def fit(parity, degree):
    nodes = 0.5 * np.cos(np.pi * (np.arange(400) + 0.5) / 800)
    turns = 2 * np.pi * nodes
    value = np.sin(turns) if parity else np.cos(turns)
    powers = np.stack([nodes ** (parity + 2 * i) for i in range(degree)], axis=1)
    return [float(c) for c in np.linalg.lstsq(powers, value, rcond=None)[0]]


SIN = fit(1, 6)
COS = fit(0, 7)


def horner(square, coefs):
    total = coefs[-1]
    for c in coefs[-2::-1]:
        total = total * square + c
    return total


def cos_sin(turns):
    r = turns - jnp.round(turns)
    square = r * r
    return horner(square, COS), horner(square, SIN) * r


def lanes(rows, length):
    return lax.broadcasted_iota(jnp.int32, (rows, length), 1)


def halves_packed(top, bottom, upper):
    length = top.shape[-1]
    half = length // 2
    low = lanes(top.shape[0], length) < half
    if upper:
        return jnp.where(low, pltpu.roll(top, half, 1), bottom)
    return jnp.where(low, top, pltpu.roll(bottom, half, 1))


def block(table_ref, s, kind):
    re, im, neg = table_ref[s, 0], table_ref[s, 1], table_ref[s, 2]
    top, bottom = ((re, neg), (im, re)) if kind == "L" else ((re, im), (neg, re))
    return jnp.concatenate(
        [jnp.concatenate(top, axis=1), jnp.concatenate(bottom, axis=1)], axis=0
    )


def piece(array, q, count, half_rows):
    groups = count // 2
    rows = 2 * half_rows
    start = pl.multiple_of(lax.rem(q, groups) * rows, half_rows)
    top = array[pl.ds(start, half_rows), :]
    bottom = array[pl.ds(start + half_rows, half_rows), :]
    return jnp.where(
        q < groups, halves_packed(top, bottom, False), halves_packed(top, bottom, True)
    )


def first_kernel(
    spectrum_any, wave_any, edge_any, band_any, maps_any, probe_any, offsets_any, measured_any,
    table, coef, probe, near, own, far_edge, total_edge, left_root, right_root,
    spectrum, wave_index, edge_band, band_coef, maps, packed, offsets, measured, sems,
):
    copies = [
        pltpu.make_async_copy(source, target, sems.at[i])
        for i, (source, target) in enumerate(
            (
                (wave_any, wave_index),
                (edge_any, edge_band),
                (band_any, band_coef),
                (spectrum_any, spectrum),
                (maps_any, maps),
                (probe_any, probe),
                (offsets_any, offsets),
                (measured_any, measured),
            )
        )
    ]
    for copy in copies:
        copy.start()
    materials, length, _ = maps.shape
    half = length // 2
    slots = probe.shape[0]
    group = 8
    centred_lane = (lanes(group, length) - half).astype(f32)
    row = lax.broadcasted_iota(jnp.int32, (group, length), 0)
    fine = row.astype(f32) * centred_lane / length
    normaliser = 1.0 / math.sqrt(length)
    coarse_rows = length // group
    copies[0].wait()

    def tables(s, carry):
        which = jnp.full((group, length), wave_index[s], jnp.int32).astype(f32)
        sampling = 0.6 + 0.4 * which / (WAVES - 1)
        fine_cos, fine_sin = cos_sin(sampling * fine)
        fine_cos, fine_sin = fine_cos * normaliser, fine_sin * normaliser
        for base in range(0, coarse_rows, group):
            step = ((row + base) * group - half).astype(f32) * centred_lane / length
            cos, sin = cos_sin(sampling * step)
            for i in range(0, group, 2):
                parts = []
                for j in (i, i + 1):
                    c = jnp.broadcast_to(cos[j : j + 1], (group, length))
                    n = jnp.broadcast_to(sin[j : j + 1], (group, length))
                    parts.append((c * fine_cos - n * fine_sin, n * fine_cos + c * fine_sin))
                at = pl.ds((base + i) * group, 2 * group)
                re = jnp.concatenate([parts[0][0], parts[1][0]], axis=0).astype(bf16)
                positive = jnp.concatenate([parts[0][1], parts[1][1]], axis=0)
                table[s, 0, at, :] = re
                table[s, 1, at, :] = (-positive).astype(bf16)
                table[s, 2, at, :] = positive.astype(bf16)
        return carry

    lax.fori_loop(0, slots, tables, 0, unroll=6)

    for copy in copies[1:]:
        copy.wait()
    for s in range(slots):
        for m in range(materials):
            band = edge_band[m, s]
            a, b = band_coef[band, 0, m], band_coef[band, 1, m]
            coef[s, m, :] = jnp.full((length,), a * (-math.log2(math.e)), f32)
            coef[s, materials + m, :] = jnp.full((length,), b * (0.5 / math.pi), f32)
            coef[s, 2 * materials + m, :] = jnp.full((length,), a, f32)
            coef[s, 3 * materials + m, :] = jnp.full((length,), b, f32)
        coef[s, 4 * materials, :] = jnp.full((length,), spectrum[s], f32)
    left_first = offsets[0] < offsets[1]
    first, second = jnp.sqrt(measured[0]), jnp.sqrt(measured[1])
    left_root[...] = jnp.where(left_first, first, second)
    right_root[...] = jnp.where(left_first, second, first)
    for m in range(materials):
        own[m] = pltpu.roll(maps[m], half, 1)
        packed[m] = halves_packed(own[m, :half], own[m, half:], False)

    def near_object(s, carry):
        for start in range(0, half, CHUNK):
            parts = object_of(coef, s, [packed[m, start : start + CHUNK] for m in range(materials)])
            for i, part in enumerate(parts):
                near[s, i, start : start + CHUNK] = part
                near[s, i, half + start : half + start + CHUNK] = pltpu.roll(part, half, 1)
        return carry

    lax.fori_loop(0, slots, near_object, 0, unroll=6)

    @pl.when(lax.axis_index("tile") == lax.axis_size("tile") - 1)
    def _():
        total_edge[...] = jnp.zeros_like(total_edge)
        low = lanes(length, length) < half

        def step(s, carry):
            re, im, cos, sin = probe[s, 0], probe[s, 1], near[s, 0], near[s, 1]
            field = [
                (jnp.where(low, re * cos - im * sin, re), jnp.where(low, re * sin + im * cos, im))
            ]
            got = transform(block(table, s, "L"), block(table, s, "R"), field)
            far_edge[s] = got
            re, im = got[:, :length], got[:, length:]
            total_edge[...] += coef[s, 4 * materials : 4 * materials + 1] * (re * re + im * im)
            return carry

        lax.fori_loop(0, slots, step, 0, unroll=EDGE_UNROLL)


def power_kernel(count, coef, probe, own, left_root, here, power, left_out):
    left_out[...] = left_root[...]
    materials, length, _ = own.shape
    half = length // 2
    slots = probe.shape[0]
    tile, tiles = lax.axis_index("tile"), lax.axis_size("tile")
    me = lax.axis_index("wave")
    low = lanes(CHUNK, length) < half
    frames = jnp.where(
        low,
        jnp.where(tile == tiles - 1, 1.0, 2.0),
        jnp.where(tile == 0, 1.0, 2.0),
    )
    for start in range(0, length, CHUNK):
        at = slice(start, start + CHUNK)
        window = [own[m, at] for m in range(materials)]

        def add(s, total):
            absorb = None
            for m in range(materials):
                term = coef[s, m : m + 1] * window[m]
                absorb = term if absorb is None else absorb + term
            re, im = probe[s, 0, at], probe[s, 1, at]
            weight = coef[s, 4 * materials : 4 * materials + 1]
            return total + (weight * jnp.exp2(absorb + absorb)) * (re * re + im * im)

        total = lax.fori_loop(0, slots, add, jnp.zeros((CHUNK, length), f32), unroll=UNROLL)
        power[at] = frames * total
    half_rows = length // count
    for m in range(materials):
        here[m] = piece(own.at[m], me, count, half_rows)


def object_of(coef, s, window):
    materials = len(window)
    absorb, phase = None, None
    for m, w in enumerate(window):
        a = coef[s, m : m + 1] * w
        b = coef[s, materials + m : materials + m + 1] * w
        absorb = a if absorb is None else absorb + a
        phase = b if phase is None else phase + b
    damping = jnp.exp2(absorb)
    cos, sin = cos_sin(phase)
    return damping * cos, damping * sin


def transform(left, right, fields):
    length = fields[0][0].shape[0]
    stacked = jnp.concatenate(
        [jnp.concatenate([re.astype(bf16), im.astype(bf16)], axis=0) for re, im in fields], axis=1
    )
    mid = jnp.dot(left, stacked, preferred_element_type=f32).astype(bf16)
    beside = jnp.concatenate(
        [
            jnp.concatenate(
                [mid[:length, i * length : (i + 1) * length], mid[length:, i * length : (i + 1) * length]], axis=1
            )
            for i in range(len(fields))
        ],
        axis=0,
    )
    if len(fields) == 1:
        beside = jnp.concatenate([beside, beside], axis=0)
    return jnp.dot(beside, right, preferred_element_type=f32)[: len(fields) * length]


def forward_kernel(count, near, halo, probe, table, coef, power, psi, far, *rest):
    messages, (beyond, total) = rest[:count], rest[count:]
    materials, length, _ = halo.shape
    half = length // 2
    slots = probe.shape[0]
    me = lax.axis_index("wave")
    for m in range(materials):
        beyond[m] = halves_packed(halo[m, :half], halo[m, half:], False)
    total[...] = jnp.zeros_like(total)
    low = lanes(CHUNK, length) < half

    def exit_wave(s):
        for start in range(0, half, CHUNK):
            parts = object_of(coef, s, [beyond[m, start : start + CHUNK] for m in range(materials)])
            upper, lower = slice(start, start + CHUNK), slice(half + start, half + start + CHUNK)
            for at, turned in ((upper, True), (lower, False)):
                cos, sin = [
                    jnp.where(low, near[s, i, at], pltpu.roll(part, half, 1) if turned else part)
                    for i, part in enumerate(parts)
                ]
                re, im = probe[s, 0, at], probe[s, 1, at]
                psi[s, 0, at] = re * cos - im * sin
                psi[s, 1, at] = re * sin + im * cos

    def step(s, joined):
        exit_wave(s)
        re, im = psi[s, 0], psi[s, 1]
        if joined:
            low = lanes(length, length) < half
            re, im = jnp.where(low, probe[s, 0], re), jnp.where(low, probe[s, 1], im)
        got = transform(block(table, s, "L"), block(table, s, "R"), [(re, im)])
        far[s] = got
        re, im = got[:, :length], got[:, length:]
        total[...] += coef[s, 4 * materials : 4 * materials + 1] * (re * re + im * im)

    edge = lax.axis_index("tile") == lax.axis_size("tile") - 1

    for joined in (False, True):

        @pl.when(edge == joined)
        def _():
            lax.fori_loop(
                0, slots, lambda s, c: (step(s, joined), c)[1], 0, unroll=EDGE_UNROLL if joined else UNROLL
            )

    half_rows = length // count
    for k, message in enumerate(messages):
        message[:length] = total[...]
        message[length:] = piece(power, jnp.bitwise_xor(me, k), count, half_rows)


def add_kernel(one, other, _, out):
    out[...] = one[...] + other[...]


def backward_kernel(tiles, count, right_root, left_root, table, coef, psi, far, far_edge, *rest):
    shares, rest = rest[:count], rest[count:]
    edges, rest = rest[: count // 2], rest[count // 2 :]
    sends, rest = rest[:count], rest[count:]
    scale, shortfall, gradient, back = rest
    length = right_root.shape[0]
    materials = gradient.shape[0]
    half = length // 2
    slots = psi.shape[0]
    edge = lax.axis_index("tile") == tiles - 1
    me = lax.axis_index("wave")
    half_rows = length // count
    powers = shares[0][length:]
    for share in shares[1:]:
        powers = powers + share[length:]
    scale[...] = relax / (powers + 1.0)
    gradient[...] = jnp.zeros_like(gradient)

    def inverse(shares):
        intensity = shares[0][:length]
        for share in shares[1:]:
            intensity = intensity + share[:length]
        return lax.rsqrt(jnp.maximum(intensity, floor_level))

    def delta(s, far, at):
        factor = coef[s, 4 * materials : 4 * materials + 1] * shortfall[at : at + length]
        return factor * far[s, :, :length], factor * far[s, :, length:]

    def collect(s):
        for start in range(0, length, CHUNK):
            at = slice(start, start + CHUNK)
            re, im = psi[s, 0, at], psi[s, 1, at]
            back_re, back_im = back[at, :length], back[at, length:]
            cross_re = re * back_re + im * back_im
            cross_im = re * back_im - im * back_re
            for m in range(materials):
                a = coef[s, 2 * materials + m : 2 * materials + m + 1]
                b = coef[s, 3 * materials + m : 3 * materials + m + 1]
                gradient[m, at] += b * cross_im - a * cross_re

    @pl.when(jnp.logical_not(edge))
    def _():
        shortfall[:length] = (right_root[...] + left_root[...]) * inverse(shares) - 2.0

        def step(s, carry):
            back[...] = transform(block(table, s, "R"), block(table, s, "L"), [delta(s, far, 0)])
            collect(s)
            return carry

        lax.fori_loop(0, slots, step, 0, unroll=UNROLL)

    @pl.when(edge)
    def _():
        shortfall[:length] = left_root[...] * inverse(shares) - 1.0
        shortfall[length:] = right_root[...] * inverse(edges) - 1.0
        low = (lax.broadcasted_iota(jnp.int32, (length, 2 * length), 1) & (length - 1)) < half

        def step(s, carry):
            both = transform(
                block(table, s, "R"), block(table, s, "L"), [delta(s, far, 0), delta(s, far_edge, length)]
            )
            back[...] = jnp.where(low, both[length:], both[:length])
            collect(s)
            return carry

        lax.fori_loop(0, slots, step, 0, unroll=EDGE_UNROLL)

    for k, send in enumerate(sends):
        for m in range(materials):
            send[m] = piece(gradient.at[m], jnp.bitwise_xor(me, k), count, half_rows)


def update_kernel(count, here, scale, *refs):
    own, arrived, out = refs[0], refs[1:-1], refs[-1]
    me = lax.axis_index("wave")
    for m in range(here.shape[0]):
        total = jnp.where(me < count // 2, own[m], arrived[0][m])
        for other in arrived[1:]:
            total = total + other[m]
        out[m] = here[m] + scale[...] * total


def join_kernel(count, *refs):
    shares, out = refs[:count], refs[count]
    materials, length, _ = out.shape
    half = length // 2
    me = lax.axis_index("wave")
    half_rows = length // count
    groups = count // 2
    low = lanes(half_rows, length) < half
    for position in range(count):

        @pl.when(me == position)
        def _():
            held = lambda q: shares[q ^ position]
            for g in range(groups):
                right, left = held(g), held(g + groups)
                start = g * 2 * half_rows
                for m in range(materials):
                    r, l = right[m], left[m]
                    out[m, start : start + half_rows] = jnp.where(low, l, pltpu.roll(r, half, 1))
                    out[m, start + half_rows : start + 2 * half_rows] = jnp.where(
                        low, pltpu.roll(l, half, 1), r
                    )


def in_hbm(array):
    return pltpu.with_memory_space_constraint(array, pltpu.HBM)


def params(mib=40):
    return pltpu.CompilerParams(vmem_limit_bytes=mib * 2**20)


def per_device(tiles, count, maps, measured, offsets, probe, spectrum, wave_index, edge_band, band_coef):
    materials, length, columns = maps.shape
    slots = probe.shape[0]
    half = length // 2
    shape = jax.ShapeDtypeStruct
    half_rows = length // count
    rest = [k for k in range(1, count) if k != count // 2]
    first_order, second_order = rest[::-1] + [count // 2], [count // 2] + rest[::-1]
    square = shape((length, length), f32)
    share = shape((materials, half_rows, length), f32)

    ring = [(i, (i - 1) % tiles) for i in range(tiles)]
    halo = lax.ppermute(maps, "tile", ring)

    band_first = jnp.transpose(band_coef, (1, 0, 2))
    field = shape((slots, length, 2 * length), f32)
    table, coef, near_probe, near, own, far_edge, total_edge, left, right_root = pl.pallas_call(
        first_kernel,
        out_shape=(
            shape((slots, 3, length, length), bf16),
            shape((slots, 6 * materials, length), f32),
            shape(probe.shape, f32),
            shape(probe.shape, f32),
            shape(maps.shape, f32),
            field,
            square,
            square,
            square,
        ),
        in_specs=[ANY] * 8,
        out_specs=(VM,) * 9,
        scratch_shapes=[
            pltpu.SMEM(spectrum.shape, f32),
            pltpu.SMEM(wave_index.shape, jnp.int32),
            pltpu.SMEM(edge_band.shape[::-1], jnp.int32),
            pltpu.SMEM(band_first.shape, f32),
            pltpu.VMEM(maps.shape, f32),
            pltpu.VMEM((materials, half, length), f32),
            pltpu.SMEM(offsets.shape, jnp.int32),
            pltpu.VMEM(measured.shape, f32),
            pltpu.SemaphoreType.DMA((8,)),
        ],
        compiler_params=params(),
        cost_estimate=pl.CostEstimate(flops=10**9, bytes_accessed=2**22, transcendentals=0),
        name="tables",
    )(*map(in_hbm, (spectrum, wave_index, edge_band.T, band_first, maps, probe, offsets, measured)))
    both = ("tile", "wave")
    last = (tiles - 1) * count

    def among_last(array, k):
        return lax.ppermute(array, both, [(last + w, last + (w ^ k)) for w in range(count)])

    other_edge = among_last(total_edge, 1)
    here, power, left = pl.pallas_call(
        lambda *refs: power_kernel(count, *refs),
        out_shape=(share, square, square),
        in_specs=[VM] * 4,
        out_specs=(VM,) * 3,
        compiler_params=params(),
        name="power",
    )(coef, near_probe, own, left)
    left_root = lax.ppermute(left, "tile", ring)
    message = shape((length + half_rows, length), f32)
    psi, far, *messages = pl.pallas_call(
        lambda *refs: forward_kernel(count, *refs),
        out_shape=(shape(probe.shape, f32), field) + (message,) * count,
        in_specs=[VM] * 6,
        out_specs=(VM,) * (2 + count),
        scratch_shapes=[
            pltpu.VMEM((materials, half, length), f32),
            pltpu.VMEM((length, length), f32),
        ],
        compiler_params=params(),
        name="forward",
    )(near, halo, near_probe, table, coef, power)
    shares = [messages[0]]
    for k in first_order:
        shares.append(lax.ppermute(messages[k], "wave", [(w, w ^ k) for w in range(count)]))
    pair_edge = pl.pallas_call(
        add_kernel,
        out_shape=square,
        in_specs=[VM] * 3,
        out_specs=VM,
        compiler_params=params(),
        name="pair",
    )(total_edge, other_edge, messages[0])
    edges = [pair_edge] + [among_last(pair_edge, k) for k in range(2, count, 2)]

    *sends, scale = pl.pallas_call(
        lambda *refs: backward_kernel(tiles, count, *refs),
        out_shape=(share,) * count + (shape((half_rows, length), f32),),
        in_specs=[VM] * (7 + count + len(edges)),
        out_specs=(VM,) * (count + 1),
        scratch_shapes=[
            pltpu.VMEM((2 * length, length), f32),
            pltpu.VMEM((materials, length, length), f32),
            pltpu.VMEM((length, 2 * length), f32),
        ],
        compiler_params=params(),
        name="backward",
    )(right_root, left_root, table, coef, psi, far, far_edge, *shares, *edges)

    def owner(t, q):
        return (t + (q >= count // 2)) % tiles * count + q

    arrived = []
    for k in (0, *second_order):
        pairs = [(t * count + w, owner(t, w ^ k)) for t in range(tiles) for w in range(count)]
        arrived.append(lax.ppermute(sends[k], both, [p for p in pairs if p[0] != p[1]]))

    new = pl.pallas_call(
        lambda *refs: update_kernel(count, *refs),
        out_shape=share,
        in_specs=[VM] * (3 + count),
        out_specs=VM,
        compiler_params=params(),
        name="update",
    )(here, scale, sends[0], *arrived)

    parts = [new]
    for k in range(1, count):
        parts.append(lax.ppermute(new, "wave", [(w, w ^ k) for w in range(count)]))
    return pl.pallas_call(
        lambda *refs: join_kernel(count, *refs),
        out_shape=shape((materials, length, length), f32),
        in_specs=[VM] * count,
        out_specs=VM,
        compiler_params=params(),
        name="join",
    )(*parts)


def solution(mesh):
    in_specs = (
        P(None, None, "tile"),
        P("tile", None, None),
        P("tile"),
        P("wave", None, None, None),
        P("wave"),
        P("wave"),
        P("wave", None),
        P(),
    )
    out_specs = P(None, None, "tile")
    tiles, count = mesh.shape["tile"], mesh.shape["wave"]
    return jax.shard_map(
        lambda *args: per_device(tiles, count, *args),
        mesh=mesh,
        in_specs=in_specs,
        out_specs=out_specs,
        check_vma=False,
    )
```

```python
import math

import jax
import jax.numpy as jnp
import numpy as np
from jax import lax
from jax.experimental import pallas as pl
from jax.experimental.pallas import tpu as pltpu
from jax.sharding import PartitionSpec as P

WAVES = 48

relax = 4.0
floor_level = 1.0

UNROLL = 12
EDGE_UNROLL = 12
CHUNK = 32

VM = pl.BlockSpec(memory_space=pltpu.VMEM)
ANY = pl.BlockSpec(memory_space=pltpu.HBM)
f32 = jnp.float32
bf16 = jnp.bfloat16


def fit(parity, degree):
    nodes = 0.5 * np.cos(np.pi * (np.arange(400) + 0.5) / 800)
    turns = 2 * np.pi * nodes
    value = np.sin(turns) if parity else np.cos(turns)
    powers = np.stack([nodes ** (parity + 2 * i) for i in range(degree)], axis=1)
    return [float(c) for c in np.linalg.lstsq(powers, value, rcond=None)[0]]


SIN = fit(1, 6)
COS = fit(0, 7)


def horner(square, coefs):
    total = coefs[-1]
    for c in coefs[-2::-1]:
        total = total * square + c
    return total


def cos_sin(turns):
    r = turns - jnp.round(turns)
    square = r * r
    return horner(square, COS), horner(square, SIN) * r


def lanes(rows, length):
    return lax.broadcasted_iota(jnp.int32, (rows, length), 1)


def halves_packed(top, bottom, upper):
    length = top.shape[-1]
    half = length // 2
    low = lanes(top.shape[0], length) < half
    if upper:
        return jnp.where(low, pltpu.roll(top, half, 1), bottom)
    return jnp.where(low, top, pltpu.roll(bottom, half, 1))


def block(table_ref, s, kind):
    re, im, neg = table_ref[s, 0], table_ref[s, 1], table_ref[s, 2]
    top, bottom = ((re, neg), (im, re)) if kind == "L" else ((re, im), (neg, re))
    return jnp.concatenate(
        [jnp.concatenate(top, axis=1), jnp.concatenate(bottom, axis=1)], axis=0
    )


def piece(array, q, count, half_rows):
    groups = count // 2
    rows = 2 * half_rows
    start = pl.multiple_of(lax.rem(q, groups) * rows, half_rows)
    top = array[pl.ds(start, half_rows), :]
    bottom = array[pl.ds(start + half_rows, half_rows), :]
    return jnp.where(
        q < groups, halves_packed(top, bottom, False), halves_packed(top, bottom, True)
    )


def first_kernel(
    spectrum_any, wave_any, edge_any, band_any, maps_any, probe_any, offsets_any, measured_any,
    table, coef, probe, near, own, far_edge, total_edge, left_root, right_root,
    spectrum, wave_index, edge_band, band_coef, maps, packed, offsets, measured, sems,
):
    copies = [
        pltpu.make_async_copy(source, target, sems.at[i])
        for i, (source, target) in enumerate(
            (
                (wave_any, wave_index),
                (edge_any, edge_band),
                (band_any, band_coef),
                (spectrum_any, spectrum),
                (maps_any, maps),
                (probe_any, probe),
                (offsets_any, offsets),
                (measured_any, measured),
            )
        )
    ]
    for copy in copies:
        copy.start()
    materials, length, _ = maps.shape
    half = length // 2
    slots = probe.shape[0]
    group = 8
    centred_lane = (lanes(group, length) - half).astype(f32)
    row = lax.broadcasted_iota(jnp.int32, (group, length), 0)
    fine = row.astype(f32) * centred_lane / length
    normaliser = 1.0 / math.sqrt(length)
    coarse_rows = length // group
    copies[0].wait()

    def tables(s, carry):
        which = jnp.full((group, length), wave_index[s], jnp.int32).astype(f32)
        sampling = 0.6 + 0.4 * which / (WAVES - 1)
        fine_cos, fine_sin = cos_sin(sampling * fine)
        fine_cos, fine_sin = fine_cos * normaliser, fine_sin * normaliser
        for base in range(0, coarse_rows, group):
            step = ((row + base) * group - half).astype(f32) * centred_lane / length
            cos, sin = cos_sin(sampling * step)
            for i in range(0, group, 2):
                parts = []
                for j in (i, i + 1):
                    c = jnp.broadcast_to(cos[j : j + 1], (group, length))
                    n = jnp.broadcast_to(sin[j : j + 1], (group, length))
                    parts.append((c * fine_cos - n * fine_sin, n * fine_cos + c * fine_sin))
                at = pl.ds((base + i) * group, 2 * group)
                re = jnp.concatenate([parts[0][0], parts[1][0]], axis=0).astype(bf16)
                positive = jnp.concatenate([parts[0][1], parts[1][1]], axis=0)
                table[s, 0, at, :] = re
                table[s, 1, at, :] = (-positive).astype(bf16)
                table[s, 2, at, :] = positive.astype(bf16)
        return carry

    lax.fori_loop(0, slots, tables, 0, unroll=6)

    for copy in copies[1:]:
        copy.wait()
    for s in range(slots):
        for m in range(materials):
            band = edge_band[m, s]
            a, b = band_coef[band, 0, m], band_coef[band, 1, m]
            coef[s, m, :] = jnp.full((length,), a * (-math.log2(math.e)), f32)
            coef[s, materials + m, :] = jnp.full((length,), b * (0.5 / math.pi), f32)
            coef[s, 2 * materials + m, :] = jnp.full((length,), a, f32)
            coef[s, 3 * materials + m, :] = jnp.full((length,), b, f32)
        coef[s, 4 * materials, :] = jnp.full((length,), spectrum[s], f32)
    left_first = offsets[0] < offsets[1]
    first, second = jnp.sqrt(measured[0]), jnp.sqrt(measured[1])
    left_root[...] = jnp.where(left_first, first, second)
    right_root[...] = jnp.where(left_first, second, first)
    for m in range(materials):
        own[m] = pltpu.roll(maps[m], half, 1)
        packed[m] = halves_packed(own[m, :half], own[m, half:], False)

    def near_object(s, carry):
        for start in range(0, half, CHUNK):
            parts = object_of(coef, s, [packed[m, start : start + CHUNK] for m in range(materials)])
            for i, part in enumerate(parts):
                near[s, i, start : start + CHUNK] = part
                near[s, i, half + start : half + start + CHUNK] = pltpu.roll(part, half, 1)
        return carry

    lax.fori_loop(0, slots, near_object, 0, unroll=6)

    @pl.when(lax.axis_index("tile") == lax.axis_size("tile") - 1)
    def _():
        total_edge[...] = jnp.zeros_like(total_edge)
        low = lanes(length, length) < half

        def step(s, carry):
            re, im, cos, sin = probe[s, 0], probe[s, 1], near[s, 0], near[s, 1]
            field = [
                (jnp.where(low, re * cos - im * sin, re), jnp.where(low, re * sin + im * cos, im))
            ]
            got = transform(block(table, s, "L"), block(table, s, "R"), field)
            far_edge[s] = got
            re, im = got[:, :length], got[:, length:]
            total_edge[...] += coef[s, 4 * materials : 4 * materials + 1] * (re * re + im * im)
            return carry

        lax.fori_loop(0, slots, step, 0, unroll=EDGE_UNROLL)


def power_kernel(count, coef, probe, own, left_root, here, power, left_out):
    left_out[...] = left_root[...]
    materials, length, _ = own.shape
    half = length // 2
    slots = probe.shape[0]
    tile, tiles = lax.axis_index("tile"), lax.axis_size("tile")
    me = lax.axis_index("wave")
    low = lanes(CHUNK, length) < half
    frames = jnp.where(
        low,
        jnp.where(tile == tiles - 1, 1.0, 2.0),
        jnp.where(tile == 0, 1.0, 2.0),
    )
    for start in range(0, length, CHUNK):
        at = slice(start, start + CHUNK)
        window = [own[m, at] for m in range(materials)]

        def add(s, total):
            absorb = None
            for m in range(materials):
                term = coef[s, m : m + 1] * window[m]
                absorb = term if absorb is None else absorb + term
            re, im = probe[s, 0, at], probe[s, 1, at]
            weight = coef[s, 4 * materials : 4 * materials + 1]
            return total + (weight * jnp.exp2(absorb + absorb)) * (re * re + im * im)

        total = lax.fori_loop(0, slots, add, jnp.zeros((CHUNK, length), f32), unroll=UNROLL)
        power[at] = frames * total
    half_rows = length // count
    for m in range(materials):
        here[m] = piece(own.at[m], me, count, half_rows)


def object_of(coef, s, window):
    materials = len(window)
    absorb, phase = None, None
    for m, w in enumerate(window):
        a = coef[s, m : m + 1] * w
        b = coef[s, materials + m : materials + m + 1] * w
        absorb = a if absorb is None else absorb + a
        phase = b if phase is None else phase + b
    damping = jnp.exp2(absorb)
    cos, sin = cos_sin(phase)
    return damping * cos, damping * sin


def transform(left, right, fields):
    length = fields[0][0].shape[0]
    stacked = jnp.concatenate(
        [jnp.concatenate([re.astype(bf16), im.astype(bf16)], axis=0) for re, im in fields], axis=1
    )
    mid = jnp.dot(left, stacked, preferred_element_type=f32).astype(bf16)
    beside = jnp.concatenate(
        [
            jnp.concatenate(
                [mid[:length, i * length : (i + 1) * length], mid[length:, i * length : (i + 1) * length]], axis=1
            )
            for i in range(len(fields))
        ],
        axis=0,
    )
    if len(fields) == 1:
        beside = jnp.concatenate([beside, beside], axis=0)
    return jnp.dot(beside, right, preferred_element_type=f32)[: len(fields) * length]


def forward_kernel(count, near, halo, probe, table, coef, power, psi, far, *rest):
    messages, (beyond, total) = rest[:count], rest[count:]
    materials, length, _ = halo.shape
    half = length // 2
    slots = probe.shape[0]
    me = lax.axis_index("wave")
    for m in range(materials):
        beyond[m] = halves_packed(halo[m, :half], halo[m, half:], False)
    total[...] = jnp.zeros_like(total)
    low = lanes(CHUNK, length) < half

    def exit_wave(s):
        for start in range(0, half, CHUNK):
            parts = object_of(coef, s, [beyond[m, start : start + CHUNK] for m in range(materials)])
            upper, lower = slice(start, start + CHUNK), slice(half + start, half + start + CHUNK)
            for at, turned in ((upper, True), (lower, False)):
                cos, sin = [
                    jnp.where(low, near[s, i, at], pltpu.roll(part, half, 1) if turned else part)
                    for i, part in enumerate(parts)
                ]
                re, im = probe[s, 0, at], probe[s, 1, at]
                psi[s, 0, at] = re * cos - im * sin
                psi[s, 1, at] = re * sin + im * cos

    def step(s, joined):
        exit_wave(s)
        re, im = psi[s, 0], psi[s, 1]
        if joined:
            low = lanes(length, length) < half
            re, im = jnp.where(low, probe[s, 0], re), jnp.where(low, probe[s, 1], im)
        got = transform(block(table, s, "L"), block(table, s, "R"), [(re, im)])
        far[s] = got
        re, im = got[:, :length], got[:, length:]
        total[...] += coef[s, 4 * materials : 4 * materials + 1] * (re * re + im * im)

    edge = lax.axis_index("tile") == lax.axis_size("tile") - 1

    for joined in (False, True):

        @pl.when(edge == joined)
        def _():
            lax.fori_loop(
                0, slots, lambda s, c: (step(s, joined), c)[1], 0, unroll=EDGE_UNROLL if joined else UNROLL
            )

    half_rows = length // count
    for k, message in enumerate(messages):
        message[:length] = total[...]
        message[length:] = piece(power, jnp.bitwise_xor(me, k), count, half_rows)


def add_kernel(one, other, _, out):
    out[...] = one[...] + other[...]


def backward_kernel(tiles, count, right_root, left_root, table, coef, psi, far, far_edge, *rest):
    shares, rest = rest[:count], rest[count:]
    edges, rest = rest[: count // 2], rest[count // 2 :]
    sends, rest = rest[:count], rest[count:]
    scale, shortfall, gradient, back = rest
    length = right_root.shape[0]
    materials = gradient.shape[0]
    half = length // 2
    slots = psi.shape[0]
    edge = lax.axis_index("tile") == tiles - 1
    me = lax.axis_index("wave")
    half_rows = length // count
    powers = shares[0][length:]
    for share in shares[1:]:
        powers = powers + share[length:]
    scale[...] = relax / (powers + 1.0)
    gradient[...] = jnp.zeros_like(gradient)

    def inverse(shares):
        intensity = shares[0][:length]
        for share in shares[1:]:
            intensity = intensity + share[:length]
        return lax.rsqrt(jnp.maximum(intensity, floor_level))

    def delta(s, far, at):
        factor = coef[s, 4 * materials : 4 * materials + 1] * shortfall[at : at + length]
        return factor * far[s, :, :length], factor * far[s, :, length:]

    def collect(s):
        for start in range(0, length, CHUNK):
            at = slice(start, start + CHUNK)
            re, im = psi[s, 0, at], psi[s, 1, at]
            back_re, back_im = back[at, :length], back[at, length:]
            cross_re = re * back_re + im * back_im
            cross_im = re * back_im - im * back_re
            for m in range(materials):
                a = coef[s, 2 * materials + m : 2 * materials + m + 1]
                b = coef[s, 3 * materials + m : 3 * materials + m + 1]
                gradient[m, at] += b * cross_im - a * cross_re

    @pl.when(jnp.logical_not(edge))
    def _():
        shortfall[:length] = (right_root[...] + left_root[...]) * inverse(shares) - 2.0

        def step(s, carry):
            back[...] = transform(block(table, s, "R"), block(table, s, "L"), [delta(s, far, 0)])
            collect(s)
            return carry

        lax.fori_loop(0, slots, step, 0, unroll=UNROLL)

    @pl.when(edge)
    def _():
        shortfall[:length] = left_root[...] * inverse(shares) - 1.0
        shortfall[length:] = right_root[...] * inverse(edges) - 1.0
        low = (lax.broadcasted_iota(jnp.int32, (length, 2 * length), 1) & (length - 1)) < half

        def step(s, carry):
            both = transform(
                block(table, s, "R"), block(table, s, "L"), [delta(s, far, 0), delta(s, far_edge, length)]
            )
            back[...] = jnp.where(low, both[length:], both[:length])
            collect(s)
            return carry

        lax.fori_loop(0, slots, step, 0, unroll=EDGE_UNROLL)

    for k, send in enumerate(sends):
        for m in range(materials):
            send[m] = piece(gradient.at[m], jnp.bitwise_xor(me, k), count, half_rows)


def update_kernel(count, here, scale, *refs):
    own, arrived, out = refs[0], refs[1:-1], refs[-1]
    me = lax.axis_index("wave")
    for m in range(here.shape[0]):
        total = jnp.where(me < count // 2, own[m], arrived[0][m])
        for other in arrived[1:]:
            total = total + other[m]
        out[m] = here[m] + scale[...] * total


def join_kernel(count, *refs):
    shares, (whole, out, sems) = refs[:count], refs[count:]
    materials, length, _ = out.shape
    half = length // 2
    me = lax.axis_index("wave")
    half_rows = length // count
    groups = count // 2
    low = lanes(half_rows, length) < half
    for position in range(count):

        @pl.when(me == position)
        def _():
            held = lambda q: shares[q ^ position]
            for m in range(materials):
                for g in range(groups):
                    right, left = held(g), held(g + groups)
                    start = g * 2 * half_rows
                    r, l = right[m], left[m]
                    out[m, start : start + half_rows] = jnp.where(low, l, pltpu.roll(r, half, 1))
                    out[m, start + half_rows : start + 2 * half_rows] = jnp.where(
                        low, pltpu.roll(l, half, 1), r
                    )
                pltpu.make_async_copy(out.at[m], whole.at[m], sems.at[m]).start()

    for m in range(materials):
        pltpu.make_async_copy(out.at[m], whole.at[m], sems.at[m]).wait()


def in_hbm(array):
    return pltpu.with_memory_space_constraint(array, pltpu.HBM)


def params(mib=40):
    return pltpu.CompilerParams(vmem_limit_bytes=mib * 2**20)


def per_device(tiles, count, maps, measured, offsets, probe, spectrum, wave_index, edge_band, band_coef):
    materials, length, columns = maps.shape
    slots = probe.shape[0]
    half = length // 2
    shape = jax.ShapeDtypeStruct
    half_rows = length // count
    rest = [k for k in range(1, count) if k != count // 2]
    first_order, second_order = rest[::-1] + [count // 2], [count // 2] + rest[::-1]
    square = shape((length, length), f32)
    share = shape((materials, half_rows, length), f32)

    ring = [(i, (i - 1) % tiles) for i in range(tiles)]
    halo = lax.ppermute(maps, "tile", ring)

    band_first = jnp.transpose(band_coef, (1, 0, 2))
    field = shape((slots, length, 2 * length), f32)
    table, coef, near_probe, near, own, far_edge, total_edge, left, right_root = pl.pallas_call(
        first_kernel,
        out_shape=(
            shape((slots, 3, length, length), bf16),
            shape((slots, 6 * materials, length), f32),
            shape(probe.shape, f32),
            shape(probe.shape, f32),
            shape(maps.shape, f32),
            field,
            square,
            square,
            square,
        ),
        in_specs=[ANY] * 8,
        out_specs=(VM,) * 9,
        scratch_shapes=[
            pltpu.SMEM(spectrum.shape, f32),
            pltpu.SMEM(wave_index.shape, jnp.int32),
            pltpu.SMEM(edge_band.shape[::-1], jnp.int32),
            pltpu.SMEM(band_first.shape, f32),
            pltpu.VMEM(maps.shape, f32),
            pltpu.VMEM((materials, half, length), f32),
            pltpu.SMEM(offsets.shape, jnp.int32),
            pltpu.VMEM(measured.shape, f32),
            pltpu.SemaphoreType.DMA((8,)),
        ],
        compiler_params=params(),
        cost_estimate=pl.CostEstimate(flops=10**9, bytes_accessed=2**22, transcendentals=0),
        name="tables",
    )(*map(in_hbm, (spectrum, wave_index, edge_band.T, band_first, maps, probe, offsets, measured)))
    both = ("tile", "wave")
    last = (tiles - 1) * count

    def among_last(array, k):
        return lax.ppermute(array, both, [(last + w, last + (w ^ k)) for w in range(count)])

    other_edge = among_last(total_edge, 1)
    here, power, left = pl.pallas_call(
        lambda *refs: power_kernel(count, *refs),
        out_shape=(share, square, square),
        in_specs=[VM] * 4,
        out_specs=(VM,) * 3,
        compiler_params=params(),
        name="power",
    )(coef, near_probe, own, left)
    left_root = lax.ppermute(left, "tile", ring)
    message = shape((length + half_rows, length), f32)
    psi, far, *messages = pl.pallas_call(
        lambda *refs: forward_kernel(count, *refs),
        out_shape=(shape(probe.shape, f32), field) + (message,) * count,
        in_specs=[VM] * 6,
        out_specs=(VM,) * (2 + count),
        scratch_shapes=[
            pltpu.VMEM((materials, half, length), f32),
            pltpu.VMEM((length, length), f32),
        ],
        compiler_params=params(),
        name="forward",
    )(near, halo, near_probe, table, coef, power)
    shares = [messages[0]]
    for k in first_order:
        shares.append(lax.ppermute(messages[k], "wave", [(w, w ^ k) for w in range(count)]))
    pair_edge = pl.pallas_call(
        add_kernel,
        out_shape=square,
        in_specs=[VM] * 3,
        out_specs=VM,
        compiler_params=params(),
        name="pair",
    )(total_edge, other_edge, messages[0])
    edges = [pair_edge] + [among_last(pair_edge, k) for k in range(2, count, 2)]

    *sends, scale = pl.pallas_call(
        lambda *refs: backward_kernel(tiles, count, *refs),
        out_shape=(share,) * count + (shape((half_rows, length), f32),),
        in_specs=[VM] * (7 + count + len(edges)),
        out_specs=(VM,) * (count + 1),
        scratch_shapes=[
            pltpu.VMEM((2 * length, length), f32),
            pltpu.VMEM((materials, length, length), f32),
            pltpu.VMEM((length, 2 * length), f32),
        ],
        compiler_params=params(),
        name="backward",
    )(right_root, left_root, table, coef, psi, far, far_edge, *shares, *edges)

    def owner(t, q):
        return (t + (q >= count // 2)) % tiles * count + q

    arrived = []
    for k in (0, *second_order):
        pairs = [(t * count + w, owner(t, w ^ k)) for t in range(tiles) for w in range(count)]
        arrived.append(lax.ppermute(sends[k], both, [p for p in pairs if p[0] != p[1]]))

    new = pl.pallas_call(
        lambda *refs: update_kernel(count, *refs),
        out_shape=share,
        in_specs=[VM] * (3 + count),
        out_specs=VM,
        compiler_params=params(),
        name="update",
    )(here, scale, sends[0], *arrived)

    parts = [new]
    for k in range(1, count):
        parts.append(lax.ppermute(new, "wave", [(w, w ^ k) for w in range(count)]))
    return pl.pallas_call(
        lambda *refs: join_kernel(count, *refs),
        out_shape=shape((materials, length, length), f32),
        in_specs=[VM] * count,
        out_specs=ANY,
        scratch_shapes=[
            pltpu.VMEM((materials, length, length), f32),
            pltpu.SemaphoreType.DMA((materials,)),
        ],
        compiler_params=params(),
        name="join",
    )(*parts)


def solution(mesh):
    in_specs = (
        P(None, None, "tile"),
        P("tile", None, None),
        P("tile"),
        P("wave", None, None, None),
        P("wave"),
        P("wave"),
        P("wave", None),
        P(),
    )
    out_specs = P(None, None, "tile")
    tiles, count = mesh.shape["tile"], mesh.shape["wave"]
    return jax.shard_map(
        lambda *args: per_device(tiles, count, *args),
        mesh=mesh,
        in_specs=in_specs,
        out_specs=out_specs,
        check_vma=False,
    )
```
